32 devices in a mesh: seq: 16 (over z, y, x), mp: 2 (over core).
Axes of the slice: x: 2, y: 2, z: 4, core: 2. Of those that a mesh axis runs over, the one named last changes fastest.
Arguments:
- kv_cache: bfloat16 [32768, 8, 256], P('seq', 'mp'), may hold values from -6 to 6
- keep_list: int32 [32768], P('seq'), may hold values from 0 to 1, as said below
- drop_level: int32 [32768], P('seq'), may hold values from 0 to 15
- drop_table: float32 [4, 16], replicated, may hold values from 0.02 to 2
- req_blocks: int32 [128], replicated, may hold values from 1 to 64, 256 in all
- tenant_sizes: int32 [4], replicated, may hold values from 1 to 64, 128 in all
- queries: bfloat16 [128, 32, 128], P(None, 'mp'), may hold values from -100 to 100
- residual: bfloat16 [128, 5120], P(None, 'seq'), may hold values from -6 to 6
- w_out: bfloat16 [4096, 5120], P('mp', 'seq'), may hold values from -0.09375 to 0.09375
- norm_gain: float32 [5120], P('seq'), may hold values from 0.5 to 1.5
- w_gate: bfloat16 [5120, 32768], P(None, ('seq', 'mp')), may hold values from -0.078125 to 0.078125
- w_up: bfloat16 [5120, 32768], P(None, ('seq', 'mp')), may hold values from -0.078125 to 0.078125
- w_down: bfloat16 [32768, 5120], P(('seq', 'mp')), may hold values from -0.0625 to 0.0625
Outputs:
- summaries: bfloat16 [256, 8, 256], P('seq', 'mp')
- packed: bfloat16 [16, 1024, 8, 256], P('seq', None, 'mp')
- final: bfloat16 [128, 5120], P(None, 'seq')
The draws below stay inside these ranges and needn't reach their ends.
Inputs may be any that keep to these rules, and one draw needn't show every extreme that they name: `keep_list`: each aligned block of 128 entries keeps between 32 and 64 of them; in every draw the 2048 entries of one index of seq keep 128 // 2 of every block. `req_blocks`: blocks of each request's cache in order; they sum to 256. `tenant_sizes`: requests of each tenant in order; they sum to 128.
All inputs are finite; a program needn't handle non-finite values.
Results may differ from the reference program's by a relative error of at most 0.007.
Values may be sent and summed in bfloat16 or wider, within the bound.
No kernel may reach another device: no remote copies, remote signals or barrier semaphores. Data moves between devices by JAX's collectives and lax.ppermute only.
A program may use at most 192 MiB of HBM per device.

```python
import math
import jax
import jax.numpy as jnp
import numpy as np
from jax import lax

D = 5120
HQ = 32
KVH = 8
HD = 128
FF = 32768
BLK = 128
LEVELS = 16
TENANTS = 4
ENT_DEV = 2048
REQS = 128
E = 32768
NB = 256
MOST_BLK = 64
OWNERS = 16
NEW_DEV = 1024


def draw_keep_list(key, part):
    key_counts, key_full, key_order = jax.random.split(jax.random.fold_in(key, 11), 3)
    halves = jax.random.randint(key_counts, (NB,), BLK // 8, BLK // 4 + 1)
    full_owner = jax.random.randint(key_full, (), 1, OWNERS)
    block_owner = jnp.arange(NB) // (ENT_DEV // BLK)
    first_block = jnp.arange(NB) % (ENT_DEV // BLK) == 0
    odd_counts = 2 * jnp.minimum(halves, BLK // 4 - 1) + 1
    even_counts = 2 * halves
    counts = jnp.where(first_block, odd_counts, even_counts)
    counts = jnp.where(block_owner == full_owner, BLK // 2, counts)
    order_keys = jax.random.split(key_order, NB)
    ranks = jax.vmap(lambda order_key: jax.random.permutation(order_key, BLK))(order_keys)
    return (ranks < counts[:, None]).astype(jnp.int32).reshape(E)


def draw_queries(key, part):
    base_key = jax.random.fold_in(jax.random.fold_in(key, 23), 0)
    pick_key = jax.random.fold_in(jax.random.fold_in(key, 23), 2)
    factor_key = jax.random.fold_in(jax.random.fold_in(key, 23), 3)
    strong_count = max(2, REQS // 8)
    strong = (jax.random.permutation(pick_key, REQS) < strong_count)[:, None, None]
    large_factor = jnp.exp(jax.random.uniform(factor_key, (REQS, 1, 1), jnp.float32, jnp.log(30.0), jnp.log(58.0)))
    values = jnp.clip(jax.random.normal(base_key, (REQS, HQ, HD), jnp.float32), -6.0, 6.0)
    values = values * jnp.where(strong, large_factor, 1.0)
    return jnp.clip(values, -100.0, 100.0).astype(jnp.bfloat16)


def set_ends(values, rng, low, top_value):
    extent = values.shape
    index_at = [jax.random.randint(jax.random.fold_in(rng, axis), (), 0, extent[axis]) for axis in range(len(extent))]
    values = values.at[tuple(index_at)].set(low)
    longest = extent.index(max(extent))
    index_at[longest] = (index_at[longest] + 1) % extent[longest]
    return values.at[tuple(index_at)].set(top_value)


def raised(drawn, key, source, target, blocks, factor):
    owner, partner = [(jnp.arange(drawn.shape[dim]) // (drawn.shape[dim] // blocks)).reshape([-1 if axis == dim else 1 for axis in range(drawn.ndim)]) for dim in (source, target)]
    chosen = jax.random.permutation(key, blocks)[partner]
    strong = (owner == chosen) | (owner == (partner + blocks // 2) % blocks)
    return jnp.where(strong, factor * drawn, drawn)


def block_scale(stream_key, extent, shards, low, high):
    factor_of = 1.0
    for position, shards_of in shards:
        draws = jax.random.uniform(jax.random.fold_in(jax.random.fold_in(stream_key, 6), position), (shards_of,), jnp.float32, low / len(shards), high / len(shards))
        factor_of = factor_of * jnp.repeat(jnp.exp(draws), extent[position] // shards_of).reshape((-1,) + (1,) * (len(extent) - 1 - position))
    return factor_of


def split_up(amount, total, most, lean):
    portions = [(1 << 20) // math.isqrt(standing ** lean) + 1 for standing in range(2, amount + 1)]
    rest, given = total - most - (amount - 1), [1] * (amount - 1)
    while rest > 0:
        free = [i for i in range(amount - 1) if given[i] < most]
        mass, left = sum([portions[i] for i in free]), rest
        for i in free:
            extra = min(most - given[i], max(1, left * portions[i] // mass), rest)
            given[i] = given[i] + extra
            rest = rest - extra
    return np.array([most] + given)


def ragged(key, count, total, bound, skew):
    if count == 2:
        one = jax.random.randint(key, (), max(1, total - bound), min(bound, total - 1) + 1)
        return jnp.stack([one, total - one])
    tallies = jnp.asarray(split_up(count, total, bound, skew), jnp.int32)
    twos = (count - 1) // 2
    donor, receiver = tallies[1:1 + 2 * twos:2], tallies[2:2 + 2 * twos:2]
    margin = jnp.minimum(donor - 1, bound - receiver)
    moved = jax.random.randint(jax.random.fold_in(key, 1), (twos,), 0, 1 << 20) % (margin + 1)
    tallies = tallies.at[1:1 + 2 * twos:2].set(donor - moved).at[2:2 + 2 * twos:2].set(receiver + moved)
    return tallies[jax.random.permutation(jax.random.fold_in(key, 2), count)]


def scatter_about(rng, dims, scale, bound, cuts=(), held_as=jnp.bfloat16):
    loudness = block_scale(rng, dims, cuts, -0.22, 0.18) if cuts else 1.0
    entries = jax.random.normal(rng, dims, jnp.float32) * scale * loudness
    return jnp.minimum(jnp.maximum(entries, -bound), bound).astype(held_as)


def heavy_noise(own_key, extent, deviation, bound, cuts, heavy, kind=jnp.bfloat16):
    drawn = deviation * jax.random.normal(own_key, extent, jnp.float32)
    if cuts:
        drawn = drawn * block_scale(own_key, extent, cuts, -0.22, 0.18)
    return jnp.clip(raised(drawn, jax.random.fold_in(own_key, 3), *heavy), -bound, bound).astype(kind)


def setup_inputs(seed: int = 0) -> dict:
    splits = jax.random.split(jax.random.key(seed), 14)
    return {
        "kv_cache": scatter_about(splits[0], (E, KVH, 2 * HD), 1.0, 6.0, ((0, 16), (1, 2))),
        "keep_list": draw_keep_list(jax.random.fold_in(splits[13], 71), 0),
        "drop_level": set_ends(jax.random.randint(splits[2], (E,), 0, LEVELS), jax.random.fold_in(splits[2], 1), 0, LEVELS - 1).astype(jnp.int32),
        "drop_table": jnp.clip(jnp.exp(jax.random.uniform(splits[3], (TENANTS, LEVELS), jnp.float32, math.log(0.02), math.log(2.0))), 0.02, 2.0),
        "req_blocks": ragged(splits[4], REQS, NB, MOST_BLK, 2).astype(jnp.int32),
        "tenant_sizes": ragged(splits[5], TENANTS, REQS, REQS // 2, 1).astype(jnp.int32),
        "queries": draw_queries(jax.random.fold_in(splits[13], 71), 0),
        "residual": scatter_about(splits[7], (REQS, D), 1.0, 6.0, ((1, 16),)),
        "w_out": scatter_about(splits[8], (HQ * HD, D), (HQ * HD) ** -0.5, 0.09375, ((0, 2), (1, 16))),
        "norm_gain": jnp.clip(1.0 + 0.1 * jax.random.normal(splits[9], (D,), jnp.float32), 0.5, 1.5),
        "w_gate": scatter_about(splits[10], (D, FF), D ** -0.5, 0.078125, ((1, 32),)),
        "w_up": scatter_about(splits[11], (D, FF), D ** -0.5, 0.078125, ((1, 32),)),
        "w_down": heavy_noise(splits[12], (FF, D), FF ** -0.5, 0.0625, ((0, 32),), (0, 1, 32, 2.75)),
    }


def owner_index(positions, bounds):
    return lax.optimization_barrier(jnp.sum((positions[:, None] >= bounds[None, :]).astype(jnp.int32), axis=1)).astype(jnp.int32)

def segment_softmax(scores, values, segment_ids, segments_total):
    row_max = jnp.maximum(jax.ops.segment_max(scores, segment_ids, num_segments=segments_total), -1e+30)
    weights = jnp.exp(scores - row_max[segment_ids])
    totals = jax.ops.segment_sum(weights, segment_ids, num_segments=segments_total)
    mixed_sum = jax.ops.segment_sum(weights[:, :, None] * values[:, None, :], segment_ids, num_segments=segments_total)
    return mixed_sum / totals[:, :, None]

def reference(kv_cache, keep_list, drop_level, drop_table, req_blocks, tenant_sizes, queries, residual, w_out, norm_gain, w_gate, w_up, w_down):
    score_scale = 1.0 / math.sqrt(HD)
    block_ids = jnp.arange(NB, dtype=jnp.int32)
    block_req = owner_index(block_ids, jnp.cumsum(req_blocks).astype(jnp.int32))
    req_tenant = owner_index(jnp.arange(REQS, dtype=jnp.int32), jnp.cumsum(tenant_sizes).astype(jnp.int32))
    block_tenant = req_tenant[block_req]
    level_rows = drop_level.reshape(NB, BLK)
    weight_rows = jnp.take_along_axis(drop_table[block_tenant], level_rows, axis=1)
    keep_rows = keep_list.reshape(NB, BLK)
    drop_weight = jnp.where(keep_rows == 1, 0.0, weight_rows).astype(jnp.bfloat16)
    weight_float = drop_weight.astype(jnp.float32)
    drop_mass = lax.optimization_barrier(jnp.sum(weight_float, axis=1))
    entry_req = jnp.repeat(block_req, BLK)
    entry_bias = jnp.where(keep_list == 1, 0.0, -jnp.inf).astype(jnp.float32)
    block_bias = jnp.log(drop_mass)
    query_heads = queries.reshape(REQS, KVH, HQ // KVH, HD).astype(jnp.float32)
    all_ids = jnp.concatenate([entry_req, block_req])

    def one_head(head_index):
        head_rows = lax.dynamic_index_in_dim(kv_cache, head_index, 1, keepdims=False).astype(jnp.float32)
        numer = jnp.einsum('bi,bic->bc', weight_float, head_rows.reshape(NB, BLK, 2 * HD), precision=lax.Precision.HIGHEST)
        summary = (numer / drop_mass[:, None]).astype(jnp.bfloat16)
        summary_float = summary.astype(jnp.float32)
        head_query = lax.dynamic_index_in_dim(query_heads, head_index, 1, keepdims=False)
        entry_scores = jnp.einsum('egd,ed->eg', head_query[entry_req], head_rows[:, :HD], precision=lax.Precision.HIGHEST) * score_scale + entry_bias[:, None]
        block_scores = jnp.einsum('bgd,bd->bg', head_query[block_req], summary_float[:, :HD], precision=lax.Precision.HIGHEST) * score_scale + block_bias[:, None]
        scores = jnp.concatenate([entry_scores, block_scores], axis=0)
        values = jnp.concatenate([head_rows[:, HD:], summary_float[:, HD:]], axis=0)
        attended = segment_softmax(scores, values, all_ids, REQS)
        return (summary, attended.astype(jnp.bfloat16))
    summaries, attended = lax.map(one_head, jnp.arange(KVH, dtype=jnp.int32))
    summaries = jnp.transpose(summaries, (1, 0, 2))
    attended = jnp.transpose(attended, (1, 0, 2, 3)).reshape(REQS, HQ * HD)
    kept_rank = (jnp.cumsum(keep_list) - 1).astype(jnp.int32)
    target = jnp.where(keep_list == 1, kept_rank % OWNERS * NEW_DEV + kept_rank // OWNERS, OWNERS * NEW_DEV).astype(jnp.int32)
    packed = jnp.zeros((OWNERS * NEW_DEV, KVH, 2 * HD), jnp.bfloat16).at[target].set(kv_cache, mode='drop')
    packed = packed.reshape(OWNERS, NEW_DEV, KVH, 2 * HD)
    projected = jnp.dot(attended, w_out, preferred_element_type=jnp.float32)
    hidden_in = residual.astype(jnp.float32) + projected
    mean_square = lax.optimization_barrier(jnp.mean(hidden_in * hidden_in, axis=1, keepdims=True))
    normed = (hidden_in * lax.rsqrt(mean_square + 1e-05) * norm_gain).astype(jnp.bfloat16)
    gate = jnp.dot(normed, w_gate, preferred_element_type=jnp.float32)
    up_proj = jnp.dot(normed, w_up, preferred_element_type=jnp.float32)
    hidden = (jax.nn.silu(gate) * up_proj).astype(jnp.bfloat16)
    down_out = jnp.dot(hidden, w_down, preferred_element_type=jnp.float32)
    final = (hidden_in + down_out).astype(jnp.bfloat16)
    return (summaries, packed, final)
```

```python
import functools
import math

import jax
import jax.numpy as jnp
from jax import lax
from jax.experimental import pallas as pl
from jax.experimental.pallas import tpu as pltpu
from jax.sharding import PartitionSpec as P

BLK = 128
LANE = 128
STAT = 16
BF = jnp.bfloat16
F32 = jnp.float32
VMEM = pl.BlockSpec(memory_space=pltpu.VMEM)
SMEM = pl.BlockSpec(memory_space=pltpu.SMEM)
ANY = pl.BlockSpec(memory_space=pl.ANY)
MIB = 1 << 20


def params(mib):
    return pltpu.CompilerParams(vmem_limit_bytes=mib * MIB)


def three(value):
    hi = value.astype(BF).astype(F32)
    mid = (value - hi).astype(BF).astype(F32)
    lo = (value - hi - mid).astype(BF).astype(F32)
    return hi, mid, lo


def attend_kernel(kvl, breq, bten, table, kv_any, keep_ref, level_ref, q_ref,
                  o_ref, sum_ref, rank_ref, kv, o_scr, sum_scr, sem):
    nb = keep_ref.shape[0]
    heads = q_ref.shape[1]
    groups = heads // kvl
    rpe = 2 * kvl
    rows = BLK * rpe
    levels = table.shape[1]
    copies = []
    for b in range(nb):
        c = pltpu.make_async_copy(kv_any.at[pl.ds(b * rows, rows)], kv.at[pl.ds(b * rows, rows)], sem.at[b])
        c.start()
        copies.append(c)
    keep = keep_ref[...]
    keep_f = keep.astype(F32)
    up = (lax.broadcasted_iota(jnp.int32, (BLK, BLK), 0) <= lax.broadcasted_iota(jnp.int32, (BLK, BLK), 1))
    within = jnp.dot(keep_f.astype(BF), up.astype(F32).astype(BF), preferred_element_type=F32)
    count = jnp.broadcast_to(jnp.sum(keep_f, axis=1, keepdims=True), (nb, BLK))
    before = jnp.zeros((nb, BLK), F32)
    row_id = lax.broadcasted_iota(jnp.int32, (nb, BLK), 0)
    for b in range(nb - 1):
        before = before + jnp.where(row_id > b, count[b:b + 1], 0.0)
    rank_ref[...] = jnp.where(keep == 1, (within + before).astype(jnp.int32) - 1, -1)
    weights = []
    for b in range(nb):
        tenant = bten[b]
        level = level_ref[b:b + 1, :]
        w = jnp.zeros((1, BLK), F32)
        for j in range(levels):
            w = jnp.where(level == j, table[tenant, j], w)
        weights.append(w)
    weight = jnp.where(keep == 1, 0.0, jnp.concatenate(weights, axis=0)).astype(BF)
    mass = jnp.sum(weight.astype(F32), axis=1, keepdims=True)
    log_mass = jnp.log(mass)
    spread = (lax.broadcasted_iota(jnp.int32, (BLK, rows), 1) // rpe
              == lax.broadcasted_iota(jnp.int32, (BLK, rows), 0)).astype(F32).astype(BF)
    wide = jnp.dot(jnp.concatenate([keep_f.astype(BF), weight], axis=0), spread, preferred_element_type=F32)
    lane_in = lax.broadcasted_iota(jnp.int32, (heads, rows), 1) % rpe
    head_of = lax.broadcasted_iota(jnp.int32, (heads, rows), 0) // groups
    is_key = lane_in == head_of
    is_value = lane_in == head_of + kvl
    scale = 1.0 / math.sqrt(LANE)
    lse_all = jnp.zeros((heads, LANE), F32)
    lane_id = lax.broadcasted_iota(jnp.int32, (heads, LANE), 1)
    for b in range(nb):
        copies[b].wait()
        block = kv[b * rows:(b + 1) * rows, :]
        q = q_ref[breq[b]]
        s = lax.dot_general(q, block, (((1,), (1,)), ((), ())), preferred_element_type=F32) * scale
        valid = is_key & (wide[b:b + 1] > 0.5)
        s = jnp.where(valid, s, -1e30)
        m = jnp.max(s, axis=1, keepdims=True)
        p = jnp.where(valid, jnp.exp(s - m), 0.0)
        total = jnp.sum(p, axis=1, keepdims=True)
        p = pltpu.roll(p, kvl, 1)
        p_hi = p.astype(BF)
        p_lo = (p - p_hi.astype(F32)).astype(BF)
        w_row = wide[nb + b:nb + b + 1]
        w_key = jnp.where(is_key, w_row, 0.0).astype(BF)
        w_val = jnp.where(is_value, w_row, 0.0).astype(BF)
        left = jnp.concatenate([p_hi, p_lo, w_key, w_val], axis=0)
        out = jnp.dot(left, block, preferred_element_type=F32)
        o = out[:heads] + out[heads:2 * heads]
        s_key = (out[2 * heads:3 * heads] / mass[b:b + 1]).astype(BF).astype(F32)
        s_val = (out[3 * heads:] / mass[b:b + 1]).astype(BF).astype(F32)
        s_score = jnp.sum(q.astype(F32) * s_key, axis=1, keepdims=True) * scale + log_mass[b:b + 1]
        top = jnp.maximum(m, s_score)
        a = jnp.exp(m - top)
        e = jnp.exp(s_score - top)
        total = total * a + e
        o_scr[:, b, :] = (o * a + s_val * e) / total
        lse_all = jnp.where(lane_id == b, top + jnp.log(total), lse_all)
        for h in range(kvl):
            sum_scr[b, h:h + 1, :LANE] = s_key[h * groups:h * groups + 1]
            sum_scr[b, h:h + 1, LANE:] = s_val[h * groups:h * groups + 1]
    o_ref[:heads] = o_scr[...].astype(BF)
    sum_ref[...] = sum_scr[...].astype(BF)
    square = jnp.concatenate([lse_all, jnp.zeros((LANE - heads, LANE), F32)], axis=0)
    lse = jnp.transpose(square)[:nb]
    hi, mid, lo = three(lse)
    o_ref[heads] = (hi + pltpu.roll(mid, 32, 1) + pltpu.roll(lo, 64, 1)).astype(BF)


def attend(kv_rows, keep, level, queries, breq, bten, table, kvl):
    nb = keep.shape[0]
    heads = queries.shape[1]
    return pl.pallas_call(
        functools.partial(attend_kernel, kvl),
        out_shape=(
            jax.ShapeDtypeStruct((heads + 1, nb, LANE), BF),
            jax.ShapeDtypeStruct((nb, kvl, 2 * LANE), BF),
            jax.ShapeDtypeStruct((nb, BLK), jnp.int32),
        ),
        in_specs=[SMEM, SMEM, SMEM, ANY, VMEM, VMEM, VMEM],
        out_specs=(VMEM, VMEM, VMEM),
        scratch_shapes=[
            pltpu.VMEM(kv_rows.shape, BF),
            pltpu.VMEM((heads, nb, LANE), F32),
            pltpu.VMEM((nb, kvl, 2 * LANE), F32),
            pltpu.SemaphoreType.DMA((nb,)),
        ],
        compiler_params=params(24),
        cost_estimate=pl.CostEstimate(flops=nb * 2 * 80 * 1024 * 128, bytes_accessed=5 * MIB, transcendentals=nb * 16384),
        name="attend",
    )(breq, bten, table, kv_rows, keep, level, queries)


def compact_kernel(dst, kv_any, out_any, kv, out, sem, out_sem):
    nb = dst.shape[0]
    slots = out_any.shape[0]
    for b in range(nb):
        pltpu.make_async_copy(kv_any.at[pl.ds(b * BLK, BLK)], kv.at[pl.ds(b * BLK, BLK)], sem.at[b]).start()

    def one(b, carry):
        pltpu.make_async_copy(kv_any.at[pl.ds(b * BLK, BLK)], kv.at[pl.ds(b * BLK, BLK)], sem.at[b]).wait()
        for i in range(BLK):
            out[dst[b, i]] = kv[b * BLK + i]
        return carry

    lax.fori_loop(0, nb, one, 0)
    copy = pltpu.make_async_copy(out.at[pl.ds(0, slots)], out_any, out_sem)
    copy.start()
    copy.wait()


def compact(kv_entries, dst, slots):
    nb = dst.shape[0]
    rpe = kv_entries.shape[1]
    return pl.pallas_call(
        compact_kernel,
        out_shape=jax.ShapeDtypeStruct((slots, rpe, LANE), BF),
        in_specs=[SMEM, ANY],
        out_specs=ANY,
        scratch_shapes=[
            pltpu.VMEM(kv_entries.shape, BF),
            pltpu.VMEM((slots + 8, rpe, LANE), BF),
            pltpu.SemaphoreType.DMA((nb,)),
            pltpu.SemaphoreType.DMA,
        ],
        compiler_params=params(16),
        cost_estimate=pl.CostEstimate(flops=0, bytes_accessed=16 * MIB, transcendentals=0),
        name="compact",
    )(dst, kv_entries)


def place_kernel(start, count, total, in_any, out_any, zeros, sem, zero_sem):
    sources, chunk = in_any.shape[0], in_any.shape[1]
    slots = out_any.shape[0]
    zeros[...] = jnp.zeros(zeros.shape, zeros.dtype)

    def piece(s):
        n = count[s]
        return pltpu.make_async_copy(in_any.at[s, pl.ds(0, n)], out_any.at[pl.ds(start[s], n)], sem.at[s])

    def blank(j):
        first = jnp.maximum(total[0], j * chunk)
        n = (j + 1) * chunk - first
        return n, lambda: pltpu.make_async_copy(zeros.at[pl.ds(0, n)], out_any.at[pl.ds(first, n)], zero_sem.at[j])

    for s in range(sources):
        pl.when(count[s] > 0)(lambda s=s: piece(s).start())
    for j in range(slots // chunk):
        n, made = blank(j)
        pl.when(n > 0)(lambda made=made: made().start())
    for s in range(sources):
        pl.when(count[s] > 0)(lambda s=s: piece(s).wait())
    for j in range(slots // chunk):
        n, made = blank(j)
        pl.when(n > 0)(lambda made=made: made().wait())


def place(incoming, start, count, total):
    sources, chunk, rpe, _ = incoming.shape
    slots = sources * chunk
    return pl.pallas_call(
        place_kernel,
        out_shape=jax.ShapeDtypeStruct((slots, rpe, LANE), BF),
        in_specs=[SMEM, SMEM, SMEM, ANY],
        out_specs=ANY,
        scratch_shapes=[
            pltpu.VMEM((chunk, rpe, LANE), BF),
            pltpu.SemaphoreType.DMA((sources,)),
            pltpu.SemaphoreType.DMA((slots // chunk,)),
        ],
        cost_estimate=pl.CostEstimate(flops=0, bytes_accessed=4 * MIB, transcendentals=0),
        name="place",
    )(start, count, total, incoming)


def strides(size):
    inner = max(size // 4, 1)
    return [j * inner for j in range(size // inner)], list(range(inner))


def swap(value, axis, size, distance):
    return lax.ppermute(value, axis, [(i, i ^ distance) for i in range(size)])


def gather_xor(value, size):
    outer, inner = strides(size)
    near = jnp.stack([value if d == 0 else swap(value, "seq", size, d) for d in outer])
    return [near if k == 0 else swap(near, "seq", size, k) for k in inner]


def relative(size, own, position):
    outer, inner = strides(size)
    n = len(outer)
    return own ^ ((position % n) * len(inner)) ^ (position // n)


def project_kernel(size, halves, place_ref, ends_ref, starts_ref, w_ref, *refs):
    parts = refs[:len(strides(size)[1])]
    outs, (att, full) = refs[len(parts):-2], refs[-2:]
    heads = parts[0].shape[1] - 1
    nb = parts[0].shape[2]
    blocks = size * nb
    requests = ends_ref.shape[1]
    own, half = place_ref[0], place_ref[1]
    at = lax.broadcasted_iota(jnp.int32, (blocks, requests), 0)
    ids = relative(size, own, at // nb) * nb + at % nb
    member = (ids >= starts_ref[...]) & (ids < ends_ref[...])
    packed = jnp.concatenate([part[:, heads].reshape(-1, LANE) for part in parts], axis=0).astype(F32)
    lse = packed + pltpu.roll(packed, LANE - 32, 1) + pltpu.roll(packed, LANE - 64, 1)
    for g in range(heads):
        column = jnp.where(member, lse[:, g:g + 1], -1e30)
        top = jnp.max(column, axis=0, keepdims=True)
        weight = jnp.where(member, jnp.exp(column - top), 0.0).astype(BF)
        total = jnp.sum(weight.astype(F32), axis=0, keepdims=True)
        o = jnp.concatenate([part[:, g].reshape(-1, LANE) for part in parts], axis=0)
        mixed = lax.dot_general(o, weight, (((0,), (0,)), ((), ())), preferred_element_type=F32)
        att[g * LANE:(g + 1) * LANE, :] = (mixed / total).astype(BF)
    full[...] = jnp.dot(w_ref[...], att[...], preferred_element_type=F32)
    if halves == 2:
        n = full.shape[0] // 2
        outs[0][...] = full[pl.ds(pl.multiple_of(half * n, 8), n), :]
        outs[1][...] = full[pl.ds(pl.multiple_of((1 - half) * n, 8), n), :]
    else:
        outs[0][...] = full[...]


def project(size, halves, where, ends, starts, w_out_t, parts):
    width, depth = w_out_t.shape
    requests = ends.shape[1]
    outs = tuple(jax.ShapeDtypeStruct((width // halves, requests), F32) for _ in range(halves))
    return pl.pallas_call(
        functools.partial(project_kernel, size, halves),
        out_shape=outs,
        in_specs=[SMEM] + [VMEM] * (3 + len(parts)),
        out_specs=tuple(VMEM for _ in outs),
        scratch_shapes=[pltpu.VMEM((depth, requests), BF), pltpu.VMEM((width, requests), F32)],
        compiler_params=params(24),
        cost_estimate=pl.CostEstimate(flops=2 * 128 * 2048 * 600, bytes_accessed=3 * MIB, transcendentals=16 * 32768),
        name="project",
    )(where, ends, starts, w_out_t, *parts)


def stream_kernel(halves, place_ref, res_ref, gain_ref, *refs):
    terms, (hidden_ref, msg_ref) = refs[:-2], refs[-2:]
    n = hidden_ref.shape[0]
    first = pl.multiple_of(place_ref[1] * n, 16) if halves == 2 else 0
    hidden = res_ref[pl.ds(first, n), :].astype(F32)
    for term in terms:
        hidden = hidden + term[...]
    hidden_ref[...] = hidden
    msg_ref[:n, :] = (hidden * gain_ref[pl.ds(first, n), :]).astype(BF)
    squares = jnp.sum(hidden * hidden, axis=0, keepdims=True)
    row = lax.broadcasted_iota(jnp.int32, (STAT, hidden.shape[1]), 0)
    stat = jnp.zeros((STAT, hidden.shape[1]), F32)
    for j, part in enumerate(three(squares)):
        stat = jnp.where(row == j, part, stat)
    msg_ref[n:, :] = stat.astype(BF)


def stream(halves, where, residual_t, gain_wide, terms):
    n, requests = terms[0].shape
    return pl.pallas_call(
        functools.partial(stream_kernel, halves),
        out_shape=(jax.ShapeDtypeStruct((n, requests), F32), jax.ShapeDtypeStruct((n + STAT, requests), BF)),
        in_specs=[SMEM] + [VMEM] * (2 + len(terms)),
        out_specs=(VMEM, VMEM),
        cost_estimate=pl.CostEstimate(flops=n * 512, bytes_accessed=MIB // 2, transcendentals=0),
        name="stream",
    )(where, residual_t, gain_wide, *terms)


def swiglu_kernel(size, halves, chunk, place_ref, gate_any, up_any, down_any, *refs):
    n_in = len(strides(size)[1])
    msgs = [refs[h * n_in:(h + 1) * n_in] for h in range(halves)]
    outs = [refs[(halves + h) * n_in:(halves + h + 1) * n_in] for h in range(halves)]
    gate, up, down, x, xt, acc_g, acc_u, h_scr, full, sem = refs[2 * halves * n_in:]
    width, units = gate.shape
    requests = x.shape[1]
    pieces = width // chunk
    n_outer = len(strides(size)[0])
    own, half = place_ref[0], place_ref[1]
    n = msgs[0][0].shape[1] - STAT

    def copies(i):
        at = pl.ds(i * chunk if isinstance(i, int) else pl.multiple_of(i * chunk, chunk), chunk)
        return (pltpu.make_async_copy(gate_any.at[at], gate.at[at], sem.at[0, i]),
                pltpu.make_async_copy(up_any.at[at], up.at[at], sem.at[1, i]))

    def down_copy(i):
        at = pl.ds(i * chunk if isinstance(i, int) else pl.multiple_of(i * chunk, chunk), chunk)
        return pltpu.make_async_copy(down_any.at[:, at], down.at[:, at], sem.at[2, i])

    for i in range(pieces):
        for c in copies(i):
            c.start()
    for i in range(pieces):
        down_copy(i).start()

    squares = jnp.zeros((1, requests), F32)
    for h in range(halves):
        side = half if h == 0 else 1 - half
        for k in range(n_in):
            for j in range(n_outer):
                s = relative(size, own, k * n_outer + j)
                at = s * (n * halves) + (side * n if halves == 2 else 0)
                x[pl.ds(pl.multiple_of(at, 16), n), :] = msgs[h][k][j, :n, :]
                stat = msgs[h][k][j, n:, :].astype(F32)
                squares = squares + jnp.sum(stat, axis=0, keepdims=True)
    scale = lax.rsqrt(squares / width + 1e-05)
    column = jnp.transpose(jnp.broadcast_to(scale, (requests, requests)))[:, :1]
    for i in range(width // LANE):
        xt[:, i * LANE:(i + 1) * LANE] = jnp.transpose(x[i * LANE:(i + 1) * LANE, :])
    acc_g[...] = jnp.zeros_like(acc_g)
    acc_u[...] = jnp.zeros_like(acc_u)

    def lap(i, carry):
        for c in copies(i):
            c.wait()
        at = pl.ds(pl.multiple_of(i * chunk, chunk), chunk)
        acc_g[...] += jnp.dot(xt[:, at], gate[at, :], preferred_element_type=F32)
        acc_u[...] += jnp.dot(xt[:, at], up[at, :], preferred_element_type=F32)
        return carry

    lax.fori_loop(0, pieces, lap, 0)
    g = acc_g[...] * column
    h_scr[...] = (g / (1.0 + jnp.exp(-g)) * (acc_u[...] * column)).astype(BF)

    def lap_down(i, carry):
        down_copy(i).wait()
        at = pl.ds(pl.multiple_of(i * chunk, chunk), chunk)
        full[at, :] = jnp.transpose(jnp.dot(h_scr[...], down[:, at], preferred_element_type=F32))
        return carry

    lax.fori_loop(0, pieces, lap_down, 0)
    for h in range(halves):
        side = half if h == 0 else 1 - half
        for k in range(n_in):
            for j in range(n_outer):
                s = relative(size, own, k * n_outer + j)
                at = s * (n * halves) + (side * n if halves == 2 else 0)
                outs[h][k][j] = full[pl.ds(pl.multiple_of(at, 8), n), :].astype(outs[h][k].dtype)


def swiglu(size, halves, where, w_gate, w_up, w_down, messages):
    outer, inner = strides(size)
    width, units = w_gate.shape
    requests = messages[0].shape[-1]
    n = messages[0].shape[1] - STAT
    chunk = 512
    outs = tuple(
        jax.ShapeDtypeStruct((len(outer), n, requests), F32 if h == 0 else BF) for h in range(halves) for _ in inner
    )
    return pl.pallas_call(
        functools.partial(swiglu_kernel, size, halves, chunk),
        out_shape=outs,
        in_specs=[SMEM, ANY, ANY, ANY] + [VMEM] * len(messages),
        out_specs=tuple(VMEM for _ in outs),
        scratch_shapes=[
            pltpu.VMEM((width, units), BF),
            pltpu.VMEM((width, units), BF),
            pltpu.VMEM((units, width), BF),
            pltpu.VMEM((width, requests), BF),
            pltpu.VMEM((requests, width), BF),
            pltpu.VMEM((requests, units), F32),
            pltpu.VMEM((requests, units), F32),
            pltpu.VMEM((requests, units), BF),
            pltpu.VMEM((width, requests), F32),
            pltpu.SemaphoreType.DMA((3, width // chunk)),
        ],
        compiler_params=params(56),
        cost_estimate=pl.CostEstimate(
            flops=6 * requests * width * units, bytes_accessed=6 * width * units, transcendentals=requests * units
        ),
        name="swiglu",
    )(where, w_gate, w_up, w_down, *messages)


def shards(
    kv_cache,
    keep_list,
    drop_level,
    drop_table,
    req_blocks,
    tenant_sizes,
    queries,
    residual,
    w_out,
    norm_gain,
    w_gate,
    w_up,
    w_down,
):
    entries, kvl, _ = kv_cache.shape
    requests = queries.shape[0]
    size = lax.axis_size("seq")
    mp = lax.axis_size("mp")
    halves = 2 if mp == 2 else 1
    own = lax.axis_index("seq")
    half = lax.axis_index("mp")
    where = jnp.stack([own, half]).astype(jnp.int32)
    nb = entries // BLK
    slots = entries // 2
    chunk = slots // size
    keep = keep_list.reshape(nb, BLK)
    level = drop_level.reshape(nb, BLK)
    by_entry = kv_cache.reshape(entries, kvl, 2, LANE).transpose(0, 2, 1, 3).reshape(entries, 2 * kvl, LANE)
    by_row = by_entry.reshape(entries * 2 * kvl, LANE)

    kept = jnp.sum(keep_list)
    counts = lax.all_to_all(jnp.broadcast_to(kept, (size,)), "seq", split_axis=0, concat_axis=0, tiled=True)
    seq_ids = jnp.arange(size, dtype=jnp.int32)
    offsets = jnp.sum(jnp.where(seq_ids[None, :] < seq_ids[:, None], counts[None, :], 0), axis=1)
    offset = jnp.sum(jnp.where(seq_ids < own, counts, 0))

    request_ids = jnp.arange(requests, dtype=jnp.int32)
    ends = jnp.sum(jnp.where(request_ids[None, :] <= request_ids[:, None], req_blocks[None, :], 0), axis=1)
    starts = ends - req_blocks
    block_ids = own * nb + jnp.arange(nb, dtype=jnp.int32)
    block_req = jnp.sum((block_ids[:, None] >= ends[None, :]).astype(jnp.int32), axis=1)
    tenants = tenant_sizes.shape[0]
    tenant_ids = jnp.arange(tenants, dtype=jnp.int32)
    tenant_ends = jnp.sum(jnp.where(tenant_ids[None, :] <= tenant_ids[:, None], tenant_sizes[None, :], 0), axis=1)
    block_tenant = jnp.sum((block_req[:, None] >= tenant_ends[None, :]).astype(jnp.int32), axis=1)

    partial, summaries, rank = attend(by_row, keep, level, queries, block_req, block_tenant, drop_table, kvl)

    position = offset + rank
    owner = position % size
    slot = position // size - (offset + size - 1 - owner) // size
    dst = jnp.where(rank >= 0, owner * chunk + slot, slots).astype(jnp.int32)
    outgoing = compact(by_entry, dst, slots).reshape(size, chunk, 2 * kvl, LANE)
    incoming = lax.all_to_all(outgoing, "seq", split_axis=0, concat_axis=0, tiled=True)
    first = (offsets + size - 1 - own) // size
    past = (offsets + counts + size - 1 - own) // size
    filled = (jnp.sum(counts) + size - 1 - own) // size
    packed = place(incoming, first, past - first, filled.reshape(1))
    packed = packed.reshape(entries // 2, 2, kvl, LANE).transpose(0, 2, 1, 3).reshape(1, slots, kvl, 2 * LANE)

    parts = gather_xor(partial, size)
    terms = project(size, halves, where, ends.reshape(1, -1), starts.reshape(1, -1), w_out.T, parts)
    if halves == 2:
        terms = (terms[0], swap(terms[1], "mp", 2, 1))
    else:
        terms = (lax.psum(terms[0], "mp"),)
    gain_wide = jnp.broadcast_to(norm_gain[:, None], (norm_gain.shape[0], requests))
    hidden, message = stream(halves, where, residual.T, gain_wide, terms)

    messages = gather_xor(message, size)
    if halves == 2:
        messages = messages + [swap(m, "mp", 2, 1) for m in messages]
    outs = swiglu(size, halves, where, w_gate, w_up, w_down, messages)
    n_in = len(outs) // halves
    if halves == 2:
        sums = [(mine + swap(theirs, "mp", 2, 1).astype(F32)).astype(BF) for mine, theirs in zip(outs[:n_in], outs[n_in:])]
    else:
        sums = [mine.astype(BF) for mine in outs]
    outer, inner = strides(size)
    near = sums[0].astype(F32)
    for k in inner[1:]:
        near = near + swap(sums[k], "seq", size, k).astype(F32)
    sent = near.astype(BF)
    down = near[0]
    for j, d in list(enumerate(outer))[1:]:
        down = down + swap(sent[j], "seq", size, d).astype(F32)
    if halves == 2:
        final = (hidden + down).astype(BF)
        other = swap(final, "mp", 2, 1)
        final = jnp.concatenate([jnp.where(half == 0, final, other), jnp.where(half == 0, other, final)], axis=0)
    else:
        down = lax.psum(down.astype(BF), "mp").astype(F32)
        final = (hidden + down).astype(BF)
    return (summaries, packed, final.T)


def solution(mesh):
    placed = (
        P("seq", "mp", None),
        P("seq"),
        P("seq"),
        P(),
        P(),
        P(),
        P(None, "mp", None),
        P(None, "seq"),
        P("mp", "seq"),
        P("seq"),
        P(None, ("seq", "mp")),
        P(None, ("seq", "mp")),
        P(("seq", "mp"), None),
    )
    return jax.shard_map(
        shards,
        mesh=mesh,
        in_specs=placed,
        out_specs=(P("seq", "mp", None), P("seq", None, "mp", None), P(None, "seq")),
        check_vma=False,
    )
```

```python
import functools
import math

import jax
import jax.numpy as jnp
from jax import lax
from jax.experimental import pallas as pl
from jax.experimental.pallas import tpu as pltpu
from jax.sharding import PartitionSpec as P

BLK = 128
LANE = 128
STAT = 16
BF = jnp.bfloat16
F32 = jnp.float32
VMEM = pl.BlockSpec(memory_space=pltpu.VMEM)
SMEM = pl.BlockSpec(memory_space=pltpu.SMEM)
ANY = pl.BlockSpec(memory_space=pl.ANY)
MIB = 1 << 20


def params(mib):
    return pltpu.CompilerParams(vmem_limit_bytes=mib * MIB)


def three(value):
    hi = value.astype(BF).astype(F32)
    mid = (value - hi).astype(BF).astype(F32)
    lo = (value - hi - mid).astype(BF).astype(F32)
    return hi, mid, lo


def attend_kernel(kvl, place_ref, req_ref, ten_ref, table, kv_any, keep_ref, level_ref, q_ref,
                  o_ref, sum_ref, rank_ref, count_ref, kv, s_scr, left, out_scr, o_scr, sum_scr, breq, sem):
    nb = keep_ref.shape[0]
    requests, heads = q_ref.shape[0], q_ref.shape[1]
    groups = heads // kvl
    rpe = 2 * kvl
    rows = BLK * rpe
    tenants, levels = table.shape
    copies = []
    for b in range(nb):
        c = pltpu.make_async_copy(kv_any.at[pl.ds(b * rows, rows)], kv.at[pl.ds(b * rows, rows)], sem.at[b])
        c.start()
        copies.append(c)
    first = place_ref[0] * nb

    def owned(r, begin):
        end = begin + req_ref[r]

        def mark(b, carry):
            breq[b] = r
            return carry

        lax.fori_loop(jnp.maximum(begin - first, 0), jnp.minimum(end - first, nb), mark, 0)
        return end

    lax.fori_loop(0, requests, owned, jnp.int32(0))
    scale = 1.0 / math.sqrt(LANE)
    for b in range(nb):
        copies[b].wait()
        s_scr[b * heads:(b + 1) * heads, :] = lax.dot_general(
            q_ref[breq[b]], kv[b * rows:(b + 1) * rows, :], (((1,), (1,)), ((), ())), preferred_element_type=F32
        )
    keep = keep_ref[...]
    keep_f = keep.astype(F32)
    up = (lax.broadcasted_iota(jnp.int32, (BLK, BLK), 0) <= lax.broadcasted_iota(jnp.int32, (BLK, BLK), 1))
    within = jnp.dot(keep_f.astype(BF), up.astype(F32).astype(BF), preferred_element_type=F32)
    count = jnp.broadcast_to(jnp.sum(keep_f, axis=1, keepdims=True), (nb, BLK))
    before = jnp.zeros((nb, BLK), F32)
    row_id = lax.broadcasted_iota(jnp.int32, (nb, BLK), 0)
    for b in range(nb - 1):
        before = before + jnp.where(row_id > b, count[b:b + 1], 0.0)
    rank_ref[...] = jnp.where(keep == 1, (within + before).astype(jnp.int32) - 1, -1)
    count_ref[...] = (before[nb - 1:] + count[nb - 1:]).astype(jnp.int32)
    weights = []
    for b in range(nb):
        request = breq[b]
        end, tenant = ten_ref[0], jnp.int32(0)
        for t in range(1, tenants):
            tenant = tenant + (request >= end).astype(jnp.int32)
            end = end + ten_ref[t]
        level = level_ref[b:b + 1, :]
        w = jnp.zeros((1, BLK), F32)
        for j in range(levels):
            w = jnp.where(level == j, table[tenant, j], w)
        weights.append(w)
    weight = jnp.where(keep == 1, 0.0, jnp.concatenate(weights, axis=0)).astype(BF)
    mass = jnp.sum(weight.astype(F32), axis=1, keepdims=True)
    log_mass = jnp.log(mass)
    spread = (lax.broadcasted_iota(jnp.int32, (BLK, rows), 1) // rpe
              == lax.broadcasted_iota(jnp.int32, (BLK, rows), 0)).astype(F32).astype(BF)
    wide = jnp.dot(jnp.concatenate([keep_f.astype(BF), weight], axis=0), spread, preferred_element_type=F32)
    lane_in = lax.broadcasted_iota(jnp.int32, (heads, rows), 1) % rpe
    head_of = lax.broadcasted_iota(jnp.int32, (heads, rows), 0) // groups
    is_key = lane_in == head_of
    is_value = lane_in == head_of + kvl
    tops, totals = [], []
    for b in range(nb):
        s = jnp.where(is_key & (wide[b:b + 1] > 0.5), s_scr[b * heads:(b + 1) * heads, :] * scale, -1e30)
        m = jnp.max(s, axis=1, keepdims=True)
        p = jnp.exp(s - m)
        tops.append(m)
        totals.append(jnp.sum(p, axis=1, keepdims=True))
        p = pltpu.roll(p, kvl, 1)
        p_hi = p.astype(BF)
        w_row = wide[nb + b:nb + b + 1]
        left[b, :heads] = p_hi
        left[b, heads:2 * heads] = (p - p_hi.astype(F32)).astype(BF)
        left[b, 2 * heads:3 * heads] = jnp.where(is_key, w_row, 0.0).astype(BF)
        left[b, 3 * heads:] = jnp.where(is_value, w_row, 0.0).astype(BF)
    for b in range(nb):
        out_scr[b] = jnp.dot(left[b], kv[b * rows:(b + 1) * rows, :], preferred_element_type=F32)
    lse_all = jnp.zeros((heads, LANE), F32)
    lane_id = lax.broadcasted_iota(jnp.int32, (heads, LANE), 1)
    for b in range(nb):
        m, total = tops[b], totals[b]
        o = out_scr[b, :heads] + out_scr[b, heads:2 * heads]
        s_key = (out_scr[b, 2 * heads:3 * heads] / mass[b:b + 1]).astype(BF).astype(F32)
        s_val = (out_scr[b, 3 * heads:] / mass[b:b + 1]).astype(BF).astype(F32)
        s_score = jnp.sum(q_ref[breq[b]].astype(F32) * s_key, axis=1, keepdims=True) * scale + log_mass[b:b + 1]
        top = jnp.maximum(m, s_score)
        a = jnp.exp(m - top)
        e = jnp.exp(s_score - top)
        total = total * a + e
        o_scr[:, b, :] = (o * a + s_val * e) / total
        lse_all = jnp.where(lane_id == b, top + jnp.log(total), lse_all)
        for h in range(kvl):
            sum_scr[b, h:h + 1, :LANE] = s_key[h * groups:h * groups + 1]
            sum_scr[b, h:h + 1, LANE:] = s_val[h * groups:h * groups + 1]
    o_ref[:heads] = o_scr[...].astype(BF)
    sum_ref[...] = sum_scr[...].astype(BF)
    square = jnp.concatenate([lse_all, jnp.zeros((LANE - heads, LANE), F32)], axis=0)
    lse = jnp.transpose(square)[:nb]
    hi, mid, lo = three(lse)
    o_ref[heads] = (hi + pltpu.roll(mid, 32, 1) + pltpu.roll(lo, 64, 1)).astype(BF)


def attend(where, req_blocks, tenant_sizes, table, kv_rows, keep, level, queries, kvl):
    nb = keep.shape[0]
    heads = queries.shape[1]
    rows = BLK * 2 * kvl
    return pl.pallas_call(
        functools.partial(attend_kernel, kvl),
        out_shape=(
            jax.ShapeDtypeStruct((heads + 1, nb, LANE), BF),
            jax.ShapeDtypeStruct((nb, kvl, 2 * LANE), BF),
            jax.ShapeDtypeStruct((nb, BLK), jnp.int32),
            jax.ShapeDtypeStruct((1, LANE), jnp.int32),
        ),
        in_specs=[SMEM, SMEM, SMEM, SMEM, ANY, VMEM, VMEM, VMEM],
        out_specs=(VMEM, VMEM, VMEM, VMEM),
        scratch_shapes=[
            pltpu.VMEM(kv_rows.shape, BF),
            pltpu.VMEM((nb * heads, rows), F32),
            pltpu.VMEM((nb, 4 * heads, rows), BF),
            pltpu.VMEM((nb, 4 * heads, LANE), F32),
            pltpu.VMEM((heads, nb, LANE), F32),
            pltpu.VMEM((nb, kvl, 2 * LANE), F32),
            pltpu.SMEM((nb,), jnp.int32),
            pltpu.SemaphoreType.DMA((nb,)),
        ],
        compiler_params=params(24),
        cost_estimate=pl.CostEstimate(flops=nb * 2 * 80 * 1024 * 128, bytes_accessed=5 * MIB, transcendentals=nb * 16384),
        name="attend",
    )(where, req_blocks, tenant_sizes, table, kv_rows, keep, level, queries)


def compact_kernel(dst, kv_any, *refs):
    outs, (kv, out, sem, out_sem) = refs[:-4], refs[-4:]
    nb = dst.shape[0]
    slots = outs[0].shape[0]
    for b in range(nb):
        pltpu.make_async_copy(kv_any.at[pl.ds(b * BLK, BLK)], kv.at[pl.ds(b * BLK, BLK)], sem.at[b]).start()

    def one(b, carry):
        pltpu.make_async_copy(kv_any.at[pl.ds(b * BLK, BLK)], kv.at[pl.ds(b * BLK, BLK)], sem.at[b]).wait()
        for i in range(BLK):
            out[dst[b, i]] = kv[b * BLK + i]
        return carry

    lax.fori_loop(0, nb, one, 0)
    copies = [pltpu.make_async_copy(out.at[pl.ds(j * slots, slots)], ref, out_sem.at[j]) for j, ref in enumerate(outs)]
    for copy in copies:
        copy.start()
    for copy in copies:
        copy.wait()


def compact(kv_entries, dst, slots, pieces):
    nb = dst.shape[0]
    rpe = kv_entries.shape[1]
    return pl.pallas_call(
        compact_kernel,
        out_shape=(jax.ShapeDtypeStruct((slots // pieces, rpe, LANE), BF),) * pieces,
        in_specs=[SMEM, ANY],
        out_specs=(ANY,) * pieces,
        scratch_shapes=[
            pltpu.VMEM(kv_entries.shape, BF),
            pltpu.VMEM((slots + 8, rpe, LANE), BF),
            pltpu.SemaphoreType.DMA((nb,)),
            pltpu.SemaphoreType.DMA((pieces,)),
        ],
        compiler_params=params(16),
        cost_estimate=pl.CostEstimate(flops=0, bytes_accessed=16 * MIB, transcendentals=0),
        name="compact",
    )(dst, kv_entries)


def place_kernel(size, place_ref, start, total, *refs):
    parts, (out_any, got, out, sem, out_sem) = refs[:-5], refs[-5:]
    near, chunk = parts[0].shape[0], parts[0].shape[1]
    slots = out_any.shape[0]
    inner = len(parts)
    copies = []
    for k, part in enumerate(parts):
        c = pltpu.make_async_copy(part, got.at[pl.ds(k * near, near)], sem.at[k])
        c.start()
        copies.append(c)
    blank = jnp.zeros(out.shape[1:], out.dtype)

    def clear(i, carry):
        for j in range(16):
            out[i * 16 + j] = blank
        return carry

    lax.fori_loop(slots // 2 // 16, slots // 16, clear, 0)
    for c in copies:
        c.wait()

    def source(s, carry):
        apart = place_ref[0] ^ s
        at = (apart % inner) * near + apart // inner
        base = start[at]
        for i in range(chunk):
            out[base + i] = got[at, i]
        return carry

    lax.fori_loop(0, size, source, 0)
    filled = total[0]
    for i in range(chunk):
        out[filled + i] = blank
    copy = pltpu.make_async_copy(out.at[pl.ds(0, slots)], out_any, out_sem)
    copy.start()
    copy.wait()


def place(size, where, parts, start, total):
    near, chunk, rpe, _ = parts[0].shape
    slots = size * chunk
    return pl.pallas_call(
        functools.partial(place_kernel, size),
        out_shape=jax.ShapeDtypeStruct((slots, rpe, LANE), BF),
        in_specs=[SMEM, SMEM, SMEM] + [ANY] * len(parts),
        out_specs=ANY,
        scratch_shapes=[
            pltpu.VMEM((size, chunk, rpe, LANE), BF),
            pltpu.VMEM((slots + chunk, rpe, LANE), BF),
            pltpu.SemaphoreType.DMA((len(parts),)),
            pltpu.SemaphoreType.DMA,
        ],
        compiler_params=params(12),
        cost_estimate=pl.CostEstimate(flops=0, bytes_accessed=4 * MIB, transcendentals=0),
        name="place",
    )(where, start, total, *parts)


def strides(size):
    inner = max(size // 4, 1)
    return [j * inner for j in range(size // inner)], list(range(inner))


def swap(value, axis, size, distance):
    return lax.ppermute(value, axis, [(i, i ^ distance) for i in range(size)])


def gather_xor(value, size):
    outer, inner = strides(size)
    near = jnp.stack([value if d == 0 else swap(value, "seq", size, d) for d in outer])
    return [near if k == 0 else swap(near, "seq", size, k) for k in inner]


def relative(size, own, position):
    outer, inner = strides(size)
    n = len(outer)
    return own ^ ((position % n) * len(inner)) ^ (position // n)


def project_kernel(size, halves, place_ref, ends_ref, starts_ref, w_ref, *refs):
    parts = refs[:len(strides(size)[1])]
    outs, (att, full) = refs[len(parts):-2], refs[-2:]
    heads = parts[0].shape[1] - 1
    nb = parts[0].shape[2]
    blocks = size * nb
    requests = ends_ref.shape[1]
    own, half = place_ref[0], place_ref[1]
    at = lax.broadcasted_iota(jnp.int32, (blocks, requests), 0)
    ids = relative(size, own, at // nb) * nb + at % nb
    member = (ids >= starts_ref[...]) & (ids < ends_ref[...])
    packed = jnp.concatenate([part[:, heads].reshape(-1, LANE) for part in parts], axis=0).astype(F32)
    lse = packed + pltpu.roll(packed, LANE - 32, 1) + pltpu.roll(packed, LANE - 64, 1)
    for g in range(heads):
        column = jnp.where(member, lse[:, g:g + 1], -1e30)
        top = jnp.max(column, axis=0, keepdims=True)
        weight = jnp.where(member, jnp.exp(column - top), 0.0).astype(BF)
        total = jnp.sum(weight.astype(F32), axis=0, keepdims=True)
        o = jnp.concatenate([part[:, g].reshape(-1, LANE) for part in parts], axis=0)
        mixed = lax.dot_general(o, weight, (((0,), (0,)), ((), ())), preferred_element_type=F32)
        att[g * LANE:(g + 1) * LANE, :] = (mixed / total).astype(BF)
    full[...] = jnp.dot(w_ref[...], att[...], preferred_element_type=F32)
    if halves == 2:
        n = full.shape[0] // 2
        outs[0][...] = full[pl.ds(pl.multiple_of(half * n, 8), n), :]
        outs[1][...] = full[pl.ds(pl.multiple_of((1 - half) * n, 8), n), :]
    else:
        outs[0][...] = full[...]


def project(size, halves, where, ends, starts, w_out_t, parts):
    width, depth = w_out_t.shape
    requests = ends.shape[1]
    outs = tuple(jax.ShapeDtypeStruct((width // halves, requests), F32) for _ in range(halves))
    return pl.pallas_call(
        functools.partial(project_kernel, size, halves),
        out_shape=outs,
        in_specs=[SMEM] + [VMEM] * (3 + len(parts)),
        out_specs=tuple(VMEM for _ in outs),
        scratch_shapes=[pltpu.VMEM((depth, requests), BF), pltpu.VMEM((width, requests), F32)],
        compiler_params=params(24),
        cost_estimate=pl.CostEstimate(flops=2 * 128 * 2048 * 600, bytes_accessed=3 * MIB, transcendentals=16 * 32768),
        name="project",
    )(where, ends, starts, w_out_t, *parts)


def stream_kernel(halves, place_ref, res_ref, gain_ref, *refs):
    terms, (hidden_ref, msg_ref) = refs[:-2], refs[-2:]
    n = hidden_ref.shape[0]
    first = pl.multiple_of(place_ref[1] * n, 16) if halves == 2 else 0
    hidden = res_ref[pl.ds(first, n), :].astype(F32)
    for term in terms:
        hidden = hidden + term[...]
    hidden_ref[...] = hidden
    msg_ref[:n, :] = (hidden * gain_ref[pl.ds(first, n), :]).astype(BF)
    squares = jnp.sum(hidden * hidden, axis=0, keepdims=True)
    row = lax.broadcasted_iota(jnp.int32, (STAT, hidden.shape[1]), 0)
    stat = jnp.zeros((STAT, hidden.shape[1]), F32)
    for j, part in enumerate(three(squares)):
        stat = jnp.where(row == j, part, stat)
    msg_ref[n:, :] = stat.astype(BF)


def stream(halves, where, residual_t, gain_wide, terms):
    n, requests = terms[0].shape
    return pl.pallas_call(
        functools.partial(stream_kernel, halves),
        out_shape=(jax.ShapeDtypeStruct((n, requests), F32), jax.ShapeDtypeStruct((n + STAT, requests), BF)),
        in_specs=[SMEM] + [VMEM] * (2 + len(terms)),
        out_specs=(VMEM, VMEM),
        cost_estimate=pl.CostEstimate(flops=n * 512, bytes_accessed=MIB // 2, transcendentals=0),
        name="stream",
    )(where, residual_t, gain_wide, *terms)


def swiglu_kernel(size, halves, chunk, place_ref, gate_any, up_any, down_any, *refs):
    n_in = len(strides(size)[1])
    msgs = [refs[h * n_in:(h + 1) * n_in] for h in range(halves)]
    outs = [refs[(halves + h) * n_in:(halves + h + 1) * n_in] for h in range(halves)]
    gate, up, down, x, xt, acc_g, acc_u, h_scr, full, sem = refs[2 * halves * n_in:]
    width, units = gate.shape
    requests = x.shape[1]
    pieces = width // chunk
    n_outer = len(strides(size)[0])
    own, half = place_ref[0], place_ref[1]
    n = msgs[0][0].shape[1] - STAT

    def copies(i):
        at = pl.ds(i * chunk if isinstance(i, int) else pl.multiple_of(i * chunk, chunk), chunk)
        return (pltpu.make_async_copy(gate_any.at[at], gate.at[at], sem.at[0, i]),
                pltpu.make_async_copy(up_any.at[at], up.at[at], sem.at[1, i]))

    def down_copy(i):
        at = pl.ds(i * chunk if isinstance(i, int) else pl.multiple_of(i * chunk, chunk), chunk)
        return pltpu.make_async_copy(down_any.at[:, at], down.at[:, at], sem.at[2, i])

    for i in range(pieces):
        for c in copies(i):
            c.start()
    for i in range(pieces):
        down_copy(i).start()

    squares = jnp.zeros((1, requests), F32)
    for h in range(halves):
        side = half if h == 0 else 1 - half
        for k in range(n_in):
            for j in range(n_outer):
                s = relative(size, own, k * n_outer + j)
                at = s * (n * halves) + (side * n if halves == 2 else 0)
                x[pl.ds(pl.multiple_of(at, 16), n), :] = msgs[h][k][j, :n, :]
                stat = msgs[h][k][j, n:, :].astype(F32)
                squares = squares + jnp.sum(stat, axis=0, keepdims=True)
    scale = lax.rsqrt(squares / width + 1e-05)
    column = jnp.transpose(jnp.broadcast_to(scale, (requests, requests)))[:, :1]
    for i in range(width // LANE):
        xt[:, i * LANE:(i + 1) * LANE] = jnp.transpose(x[i * LANE:(i + 1) * LANE, :])
    acc_g[...] = jnp.zeros_like(acc_g)
    acc_u[...] = jnp.zeros_like(acc_u)

    def lap(i, carry):
        for c in copies(i):
            c.wait()
        at = pl.ds(pl.multiple_of(i * chunk, chunk), chunk)
        acc_g[...] += jnp.dot(xt[:, at], gate[at, :], preferred_element_type=F32)
        acc_u[...] += jnp.dot(xt[:, at], up[at, :], preferred_element_type=F32)
        return carry

    lax.fori_loop(0, pieces, lap, 0)
    g = acc_g[...] * column
    h_scr[...] = (g / (1.0 + jnp.exp(-g)) * (acc_u[...] * column)).astype(BF)

    def lap_down(i, carry):
        down_copy(i).wait()
        at = pl.ds(pl.multiple_of(i * chunk, chunk), chunk)
        full[at, :] = jnp.transpose(jnp.dot(h_scr[...], down[:, at], preferred_element_type=F32))
        return carry

    lax.fori_loop(0, pieces, lap_down, 0)
    for h in range(halves):
        side = half if h == 0 else 1 - half
        for k in range(n_in):
            for j in range(n_outer):
                s = relative(size, own, k * n_outer + j)
                at = s * (n * halves) + (side * n if halves == 2 else 0)
                outs[h][k][j] = full[pl.ds(pl.multiple_of(at, 8), n), :].astype(outs[h][k].dtype)


def swiglu(size, halves, where, w_gate, w_up, w_down, messages):
    outer, inner = strides(size)
    width, units = w_gate.shape
    requests = messages[0].shape[-1]
    n = messages[0].shape[1] - STAT
    chunk = 512
    outs = tuple(
        jax.ShapeDtypeStruct((len(outer), n, requests), F32 if h == 0 else BF) for h in range(halves) for _ in inner
    )
    return pl.pallas_call(
        functools.partial(swiglu_kernel, size, halves, chunk),
        out_shape=outs,
        in_specs=[SMEM, ANY, ANY, ANY] + [VMEM] * len(messages),
        out_specs=tuple(VMEM for _ in outs),
        scratch_shapes=[
            pltpu.VMEM((width, units), BF),
            pltpu.VMEM((width, units), BF),
            pltpu.VMEM((units, width), BF),
            pltpu.VMEM((width, requests), BF),
            pltpu.VMEM((requests, width), BF),
            pltpu.VMEM((requests, units), F32),
            pltpu.VMEM((requests, units), F32),
            pltpu.VMEM((requests, units), BF),
            pltpu.VMEM((width, requests), F32),
            pltpu.SemaphoreType.DMA((3, width // chunk)),
        ],
        compiler_params=params(56),
        cost_estimate=pl.CostEstimate(
            flops=6 * requests * width * units, bytes_accessed=6 * width * units, transcendentals=requests * units
        ),
        name="swiglu",
    )(where, w_gate, w_up, w_down, *messages)


def shards(
    kv_cache,
    keep_list,
    drop_level,
    drop_table,
    req_blocks,
    tenant_sizes,
    queries,
    residual,
    w_out,
    norm_gain,
    w_gate,
    w_up,
    w_down,
):
    entries, kvl, _ = kv_cache.shape
    requests = queries.shape[0]
    size = lax.axis_size("seq")
    mp = lax.axis_size("mp")
    halves = 2 if mp == 2 else 1
    own = lax.axis_index("seq")
    half = lax.axis_index("mp")
    where = jnp.stack([own, half]).astype(jnp.int32)
    nb = entries // BLK
    slots = entries // 2
    chunk = slots // size
    keep = keep_list.reshape(nb, BLK)
    level = drop_level.reshape(nb, BLK)
    by_entry = kv_cache.reshape(entries, kvl, 2, LANE).transpose(0, 2, 1, 3).reshape(entries, 2 * kvl, LANE)
    by_row = by_entry.reshape(entries * 2 * kvl, LANE)
    outer, inner = strides(size)
    n_outer, n_inner = len(outer), len(inner)

    partial, summaries, rank, kept = attend(
        where, req_blocks, tenant_sizes, drop_table, by_row, keep, level, queries, kvl
    )
    parts = gather_xor(partial, size)

    counts = jnp.concatenate([part[:, 0, 0] for part in gather_xor(kept, size)])
    sources = relative(size, own, jnp.arange(size, dtype=jnp.int32))
    offsets = jnp.sum(jnp.where(sources[None, :] < sources[:, None], counts[None, :], 0), axis=1)
    offset = jnp.sum(jnp.where(sources < own, counts, 0))

    position = offset + rank
    owner = position % size
    slot = position // size - (offset + size - 1 - owner) // size
    dst = jnp.where(rank >= 0, (owner ^ own) * chunk + slot, slots).astype(jnp.int32)
    outgoing = [piece.reshape(n_inner, chunk, 2 * kvl, LANE) for piece in compact(by_entry, dst, slots, n_outer)]
    across = [piece if d == 0 else swap(piece, "seq", size, d) for piece, d in zip(outgoing, outer)]
    incoming = [jnp.stack([piece[k] for piece in across]) for k in inner]
    incoming = [piece if k == 0 else swap(piece, "seq", size, k) for piece, k in zip(incoming, inner)]
    first = (offsets + size - 1 - own) // size
    filled = (jnp.sum(counts) + size - 1 - own) // size
    packed = place(size, where, incoming, first, filled.reshape(1))
    packed = packed.reshape(slots, 2, kvl, LANE).transpose(0, 2, 1, 3).reshape(1, slots, kvl, 2 * LANE)

    request_ids = jnp.arange(requests, dtype=jnp.int32)
    ends = jnp.sum(jnp.where(request_ids[None, :] <= request_ids[:, None], req_blocks[None, :], 0), axis=1)
    starts = ends - req_blocks

    terms = project(size, halves, where, ends.reshape(1, -1), starts.reshape(1, -1), w_out.T, parts)
    if halves == 2:
        terms = (terms[0], swap(terms[1], "mp", 2, 1))
    else:
        terms = (lax.psum(terms[0], "mp"),)
    gain_wide = jnp.broadcast_to(norm_gain[:, None], (norm_gain.shape[0], requests))
    hidden, message = stream(halves, where, residual.T, gain_wide, terms)

    messages = gather_xor(message, size)
    if halves == 2:
        messages = messages + [swap(m, "mp", 2, 1) for m in messages]
    outs = swiglu(size, halves, where, w_gate, w_up, w_down, messages)
    n_in = len(outs) // halves
    if halves == 2:
        sums = [(mine + swap(theirs, "mp", 2, 1).astype(F32)).astype(BF) for mine, theirs in zip(outs[:n_in], outs[n_in:])]
    else:
        sums = [mine.astype(BF) for mine in outs]
    near = sums[0].astype(F32)
    for k in inner[1:]:
        near = near + swap(sums[k], "seq", size, k).astype(F32)
    sent = near.astype(BF)
    down = near[0]
    for j, d in list(enumerate(outer))[1:]:
        down = down + swap(sent[j], "seq", size, d).astype(F32)
    if halves == 2:
        final = (hidden + down).astype(BF)
        other = swap(final, "mp", 2, 1)
        final = jnp.concatenate([jnp.where(half == 0, final, other), jnp.where(half == 0, other, final)], axis=0)
    else:
        down = lax.psum(down.astype(BF), "mp").astype(F32)
        final = (hidden + down).astype(BF)
    return (summaries, packed, final.T)


def solution(mesh):
    placed = (
        P("seq", "mp", None),
        P("seq"),
        P("seq"),
        P(),
        P(),
        P(),
        P(None, "mp", None),
        P(None, "seq"),
        P("mp", "seq"),
        P("seq"),
        P(None, ("seq", "mp")),
        P(None, ("seq", "mp")),
        P(("seq", "mp"), None),
    )
    return jax.shard_map(
        shards,
        mesh=mesh,
        in_specs=placed,
        out_specs=(P("seq", "mp", None), P("seq", None, "mp", None), P(None, "seq")),
        check_vma=False,
    )
```

```python
import functools
import math

import jax
import jax.numpy as jnp
from jax import lax
from jax.experimental import pallas as pl
from jax.experimental.pallas import tpu as pltpu
from jax.sharding import PartitionSpec as P

BLK = 128
LANE = 128
STAT = 16
BF = jnp.bfloat16
F32 = jnp.float32
VMEM = pl.BlockSpec(memory_space=pltpu.VMEM)
SMEM = pl.BlockSpec(memory_space=pltpu.SMEM)
ANY = pl.BlockSpec(memory_space=pl.ANY)
MIB = 1 << 20
SMALL = pl.CostEstimate(flops=0, bytes_accessed=1024, transcendentals=0)


def params(mib):
    return pltpu.CompilerParams(vmem_limit_bytes=mib * MIB)


def three(value):
    hi = value.astype(BF).astype(F32)
    mid = (value - hi).astype(BF).astype(F32)
    lo = (value - hi - mid).astype(BF).astype(F32)
    return hi, mid, lo


def attend_kernel(kvl, place_ref, req_ref, ten_ref, table, kv_any, keep_ref, level_ref, q_ref,
                  o_ref, sum_ref, rank_ref, kv, s_scr, left, out_scr, o_scr, sum_scr, breq, sem):
    nb = keep_ref.shape[0]
    requests, heads = q_ref.shape[0], q_ref.shape[1]
    groups = heads // kvl
    rpe = 2 * kvl
    rows = BLK * rpe
    tenants, levels = table.shape
    copies = []
    for b in range(nb):
        c = pltpu.make_async_copy(kv_any.at[pl.ds(b * rows, rows)], kv.at[pl.ds(b * rows, rows)], sem.at[b])
        c.start()
        copies.append(c)
    first = place_ref[0] * nb

    def owned(r, begin):
        end = begin + req_ref[r]

        def mark(b, carry):
            breq[b] = r
            return carry

        lax.fori_loop(jnp.maximum(begin - first, 0), jnp.minimum(end - first, nb), mark, 0)
        return end

    lax.fori_loop(0, requests, owned, jnp.int32(0))
    scale = 1.0 / math.sqrt(LANE)
    for b in range(nb):
        copies[b].wait()
        s_scr[b * heads:(b + 1) * heads, :] = lax.dot_general(
            q_ref[breq[b]], kv[b * rows:(b + 1) * rows, :], (((1,), (1,)), ((), ())), preferred_element_type=F32
        )
    keep = keep_ref[...]
    keep_f = keep.astype(F32)
    up = (lax.broadcasted_iota(jnp.int32, (BLK, BLK), 0) <= lax.broadcasted_iota(jnp.int32, (BLK, BLK), 1))
    within = jnp.dot(keep_f.astype(BF), up.astype(F32).astype(BF), preferred_element_type=F32)
    count = jnp.broadcast_to(jnp.sum(keep_f, axis=1, keepdims=True), (nb, BLK))
    before = jnp.zeros((nb, BLK), F32)
    row_id = lax.broadcasted_iota(jnp.int32, (nb, BLK), 0)
    for b in range(nb - 1):
        before = before + jnp.where(row_id > b, count[b:b + 1], 0.0)
    rank_ref[...] = jnp.where(keep == 1, (within + before).astype(jnp.int32) - 1, -1)
    weights = []
    for b in range(nb):
        request = breq[b]
        end, tenant = ten_ref[0], jnp.int32(0)
        for t in range(1, tenants):
            tenant = tenant + (request >= end).astype(jnp.int32)
            end = end + ten_ref[t]
        level = level_ref[b:b + 1, :]
        w = jnp.zeros((1, BLK), F32)
        for j in range(levels):
            w = jnp.where(level == j, table[tenant, j], w)
        weights.append(w)
    weight = jnp.where(keep == 1, 0.0, jnp.concatenate(weights, axis=0)).astype(BF)
    mass = jnp.sum(weight.astype(F32), axis=1, keepdims=True)
    log_mass = jnp.log(mass)
    spread = (lax.broadcasted_iota(jnp.int32, (BLK, rows), 1) // rpe
              == lax.broadcasted_iota(jnp.int32, (BLK, rows), 0)).astype(F32).astype(BF)
    wide = jnp.dot(jnp.concatenate([keep_f.astype(BF), weight], axis=0), spread, preferred_element_type=F32)
    lane_in = lax.broadcasted_iota(jnp.int32, (heads, rows), 1) % rpe
    head_of = lax.broadcasted_iota(jnp.int32, (heads, rows), 0) // groups
    is_key = lane_in == head_of
    is_value = lane_in == head_of + kvl
    tops, totals = [], []
    for b in range(nb):
        s = jnp.where(is_key & (wide[b:b + 1] > 0.5), s_scr[b * heads:(b + 1) * heads, :] * scale, -1e30)
        m = jnp.max(s, axis=1, keepdims=True)
        p = jnp.exp(s - m)
        tops.append(m)
        totals.append(jnp.sum(p, axis=1, keepdims=True))
        p = pltpu.roll(p, kvl, 1)
        p_hi = p.astype(BF)
        w_row = wide[nb + b:nb + b + 1]
        left[b, :heads] = p_hi
        left[b, heads:2 * heads] = (p - p_hi.astype(F32)).astype(BF)
        left[b, 2 * heads:3 * heads] = jnp.where(is_key, w_row, 0.0).astype(BF)
        left[b, 3 * heads:] = jnp.where(is_value, w_row, 0.0).astype(BF)
    for b in range(nb):
        out_scr[b] = jnp.dot(left[b], kv[b * rows:(b + 1) * rows, :], preferred_element_type=F32)
    lse_all = jnp.zeros((heads, LANE), F32)
    lane_id = lax.broadcasted_iota(jnp.int32, (heads, LANE), 1)
    for b in range(nb):
        m, total = tops[b], totals[b]
        o = out_scr[b, :heads] + out_scr[b, heads:2 * heads]
        s_key = (out_scr[b, 2 * heads:3 * heads] / mass[b:b + 1]).astype(BF).astype(F32)
        s_val = (out_scr[b, 3 * heads:] / mass[b:b + 1]).astype(BF).astype(F32)
        s_score = jnp.sum(q_ref[breq[b]].astype(F32) * s_key, axis=1, keepdims=True) * scale + log_mass[b:b + 1]
        top = jnp.maximum(m, s_score)
        a = jnp.exp(m - top)
        e = jnp.exp(s_score - top)
        total = total * a + e
        o_scr[:, b, :] = (o * a + s_val * e) / total
        lse_all = jnp.where(lane_id == b, top + jnp.log(total), lse_all)
        for h in range(kvl):
            sum_scr[b, h:h + 1, :LANE] = s_key[h * groups:h * groups + 1]
            sum_scr[b, h:h + 1, LANE:] = s_val[h * groups:h * groups + 1]
    o_ref[:heads] = o_scr[...].astype(BF)
    sum_ref[...] = sum_scr[...].astype(BF)
    square = jnp.concatenate([lse_all, jnp.zeros((LANE - heads, LANE), F32)], axis=0)
    lse = jnp.transpose(square)[:nb]
    hi, mid, lo = three(lse)
    o_ref[heads] = (hi + pltpu.roll(mid, 32, 1) + pltpu.roll(lo, 64, 1)).astype(BF)


def attend(where, req_blocks, tenant_sizes, table, kv_rows, keep, level, queries, kvl):
    nb = keep.shape[0]
    heads = queries.shape[1]
    rows = BLK * 2 * kvl
    return pl.pallas_call(
        functools.partial(attend_kernel, kvl),
        out_shape=(
            jax.ShapeDtypeStruct((heads + 1, nb, LANE), BF),
            jax.ShapeDtypeStruct((nb, kvl, 2 * LANE), BF),
            jax.ShapeDtypeStruct((nb, BLK), jnp.int32),
        ),
        in_specs=[SMEM, SMEM, SMEM, SMEM, ANY, VMEM, VMEM, VMEM],
        out_specs=(VMEM, VMEM, VMEM),
        scratch_shapes=[
            pltpu.VMEM(kv_rows.shape, BF),
            pltpu.VMEM((nb * heads, rows), F32),
            pltpu.VMEM((nb, 4 * heads, rows), BF),
            pltpu.VMEM((nb, 4 * heads, LANE), F32),
            pltpu.VMEM((heads, nb, LANE), F32),
            pltpu.VMEM((nb, kvl, 2 * LANE), F32),
            pltpu.SMEM((nb,), jnp.int32),
            pltpu.SemaphoreType.DMA((nb,)),
        ],
        compiler_params=params(60),
        cost_estimate=pl.CostEstimate(flops=nb * 2 * 80 * 1024 * 128, bytes_accessed=5 * MIB, transcendentals=nb * 16384),
        name="attend",
    )(where, req_blocks, tenant_sizes, table, kv_rows, keep, level, queries)


def shift(value, size):
    return lax.shift_right_logical(value, jnp.int32(size.bit_length() - 1))


def compact_kernel(size, early, late, place_ref, rank_ref, kv_any, *refs):
    count_refs, refs = refs[:len(strides(size)[1])], refs[len(strides(size)[1]):]
    outs, total_ref, (kv, out, dst_v, dst, sem, out_sem, dst_sem) = refs[:-8], refs[-8], refs[-7:]
    nb = rank_ref.shape[0]
    n_outer, n_inner = (len(d) for d in strides(size))
    own = place_ref[0]
    for b in range(nb):
        pltpu.make_async_copy(kv_any.at[pl.ds(b * BLK, BLK)], kv.at[pl.ds(b * BLK, BLK)], sem.at[b]).start()
    by_lane = jnp.concatenate([ref[j] for ref in count_refs for j in range(ref.shape[0])], axis=0).astype(F32)
    counts = jnp.broadcast_to(jnp.sum(by_lane, axis=1, keepdims=True), (size, LANE))
    total_ref[...] = counts.astype(jnp.int32)
    source = relative(size, own, lax.broadcasted_iota(jnp.int32, (size, LANE), 0))
    offset = jnp.sum(jnp.where(source < own, counts, 0.0), axis=0, keepdims=True).astype(jnp.int32)
    rank = rank_ref[...]
    position = offset + jnp.maximum(rank, 0)
    owner = position & (size - 1)
    slot = shift(position, size) - shift(offset + (size - 1) - owner, size)
    apart = owner ^ own
    k, j = apart & (n_inner - 1), shift(apart, n_inner)
    first = (j * n_inner + k) * early + slot
    second = size * early + (k * n_outer + j) * late + slot - early
    dst_v[...] = jnp.where(rank >= 0, jnp.where(slot < early, first, second), size * (early + late))
    to_scalars = pltpu.make_async_copy(dst_v, dst, dst_sem)
    to_scalars.start()
    to_scalars.wait()

    def one(b, carry):
        pltpu.make_async_copy(kv_any.at[pl.ds(b * BLK, BLK)], kv.at[pl.ds(b * BLK, BLK)], sem.at[b]).wait()
        for i in range(BLK):
            out[dst[b, i]] = kv[b * BLK + i]
        return carry

    lax.fori_loop(0, nb, one, 0)
    copies, at = [], 0
    for j, ref in enumerate(outs):
        copies.append(pltpu.make_async_copy(out.at[pl.ds(at, ref.shape[0])], ref, out_sem.at[j]))
        at += ref.shape[0]
    for copy in copies:
        copy.start()
    for copy in copies:
        copy.wait()


def compact(size, early, late, where, rank, counts, kv_entries):
    nb = rank.shape[0]
    rpe = kv_entries.shape[1]
    n_outer, n_inner = (len(d) for d in strides(size))
    lengths = [n_inner * early] * n_outer + [n_outer * late] * n_inner
    return pl.pallas_call(
        functools.partial(compact_kernel, size, early, late),
        out_shape=tuple(jax.ShapeDtypeStruct((n, rpe, LANE), BF) for n in lengths)
        + (jax.ShapeDtypeStruct((size, LANE), jnp.int32),),
        in_specs=[SMEM, VMEM, ANY] + [VMEM] * len(counts),
        out_specs=(ANY,) * len(lengths) + (VMEM,),
        scratch_shapes=[
            pltpu.VMEM(kv_entries.shape, BF),
            pltpu.VMEM((sum(lengths) + 8, rpe, LANE), BF),
            pltpu.VMEM((nb, BLK), jnp.int32),
            pltpu.SMEM((nb, BLK), jnp.int32),
            pltpu.SemaphoreType.DMA((nb,)),
            pltpu.SemaphoreType.DMA((len(lengths),)),
            pltpu.SemaphoreType.DMA,
        ],
        compiler_params=params(60),
        cost_estimate=SMALL,
        name="compact",
    )(where, rank, kv_entries, *counts)


def regroup_kernel(n, *refs):
    ins, outs, held, sem, out_sem = refs[:n], refs[n:-3], refs[-3], refs[-2], refs[-1]
    m = len(outs)
    copies = [[pltpu.make_async_copy(ref.at[i], held.at[i, j], sem.at[j, i]) for j, ref in enumerate(ins)] for i in range(m)]
    for row in copies:
        for copy in row:
            copy.start()
    sends = []
    for i, row in enumerate(copies):
        for copy in row:
            copy.wait()
        sends.append(pltpu.make_async_copy(held.at[i], outs[i], out_sem.at[i]))
        sends[-1].start()
    for copy in sends:
        copy.wait()


def regroup(values):
    n, m = len(values), values[0].shape[0]
    return pl.pallas_call(
        functools.partial(regroup_kernel, n),
        out_shape=(jax.ShapeDtypeStruct((n, *values[0].shape[1:]), values[0].dtype),) * m,
        in_specs=[ANY] * n,
        out_specs=(ANY,) * m,
        scratch_shapes=[
            pltpu.VMEM((m, n, *values[0].shape[1:]), values[0].dtype),
            pltpu.SemaphoreType.DMA((n, m)),
            pltpu.SemaphoreType.DMA((m,)),
        ],
        compiler_params=params(60),
        cost_estimate=SMALL,
        name="regroup",
    )(*values)


def place_kernel(size, n_inner, place_ref, count, *refs):
    parts, (out_any, got, out, sem, out_sem) = refs[:-5], refs[-5:]
    early = parts[0].shape[1]
    chunk = got.shape[2]
    slots = out_any.shape[0]
    copies = []
    for i, part in enumerate(parts):
        if i < n_inner:
            to = got.at[i, :, pl.ds(0, early)]
        else:
            to = got.at[:, i - n_inner, pl.ds(early, chunk - early)]
        c = pltpu.make_async_copy(part, to, sem.at[i])
        c.start()
        copies.append(c)
    blank = jnp.zeros(out.shape[1:], out.dtype)

    def clear(i, carry):
        for j in range(16):
            out[i * 16 + j] = blank
        return carry

    lax.fori_loop(slots // 2 // 16, slots // 16, clear, 0)
    for c in copies:
        c.wait()

    own = place_ref[0]

    def source(s, before):
        apart = own ^ s
        k, j = apart & (n_inner - 1), shift(apart, n_inner)
        base = shift(before + (size - 1) - own, size)
        for i in range(chunk):
            out[base + i] = got[k, j, i]
        return before + count[k * got.shape[1] + j, 0]

    filled = shift(lax.fori_loop(0, size, source, jnp.int32(0)) + (size - 1) - own, size)
    for i in range(chunk):
        out[filled + i] = blank
    copy = pltpu.make_async_copy(out.at[pl.ds(0, slots)], out_any, out_sem)
    copy.start()
    copy.wait()


def place(size, where, early, late, counts):
    n_outer, n_inner = len(late), len(early)
    rpe = early[0].shape[2]
    chunk = early[0].shape[1] + late[0].shape[1]
    slots = size * chunk
    return pl.pallas_call(
        functools.partial(place_kernel, size, n_inner),
        out_shape=jax.ShapeDtypeStruct((slots, rpe, LANE), BF),
        in_specs=[SMEM, SMEM] + [ANY] * (n_outer + n_inner),
        out_specs=ANY,
        scratch_shapes=[
            pltpu.VMEM((n_inner, n_outer, chunk, rpe, LANE), BF),
            pltpu.VMEM((slots + chunk, rpe, LANE), BF),
            pltpu.SemaphoreType.DMA((n_inner + n_outer,)),
            pltpu.SemaphoreType.DMA,
        ],
        compiler_params=params(12),
        cost_estimate=SMALL,
        name="place",
    )(where, counts, *early, *late)


def strides(size):
    inner = max(size // 4, 1)
    return [j * inner for j in range(size // inner)], list(range(inner))


def swap(value, axis, size, distance):
    return lax.ppermute(value, axis, [(i, i ^ distance) for i in range(size)])


def gather_near(value, size):
    return jnp.stack([value if d == 0 else swap(value, "seq", size, d) for d in strides(size)[0]])


def gather_far(near, size):
    return [near if k == 0 else swap(near, "seq", size, k) for k in strides(size)[1]]


def after(value, *others):
    return lax.optimization_barrier((value, others))[0]


def relative(size, own, position):
    outer, inner = strides(size)
    n = len(outer)
    return own ^ ((position % n) * len(inner)) ^ (position // n)


def project_kernel(size, halves, place_ref, ends_ref, starts_ref, w_ref, *refs):
    parts = refs[:len(strides(size)[1])]
    outs, (att, full) = refs[len(parts):-2], refs[-2:]
    heads = parts[0].shape[1] - 1
    nb = parts[0].shape[2]
    blocks = size * nb
    requests = ends_ref.shape[1]
    own, half = place_ref[0], place_ref[1]
    at = lax.broadcasted_iota(jnp.int32, (blocks, requests), 0)
    ids = relative(size, own, at // nb) * nb + at % nb
    member = (ids >= starts_ref[...]) & (ids < ends_ref[...])
    packed = jnp.concatenate([part[:, heads].reshape(-1, LANE) for part in parts], axis=0).astype(F32)
    lse = packed + pltpu.roll(packed, LANE - 32, 1) + pltpu.roll(packed, LANE - 64, 1)
    for g in range(heads):
        column = jnp.where(member, lse[:, g:g + 1], -1e30)
        top = jnp.max(column, axis=0, keepdims=True)
        weight = jnp.where(member, jnp.exp(column - top), 0.0).astype(BF)
        total = jnp.sum(weight.astype(F32), axis=0, keepdims=True)
        o = jnp.concatenate([part[:, g].reshape(-1, LANE) for part in parts], axis=0)
        mixed = lax.dot_general(o, weight, (((0,), (0,)), ((), ())), preferred_element_type=F32)
        att[g * LANE:(g + 1) * LANE, :] = (mixed / total).astype(BF)
    full[...] = jnp.dot(w_ref[...], att[...], preferred_element_type=F32)
    if halves == 2:
        n = full.shape[0] // 2
        outs[0][...] = full[pl.ds(pl.multiple_of(half * n, 8), n), :]
        outs[1][...] = full[pl.ds(pl.multiple_of((1 - half) * n, 8), n), :]
    else:
        outs[0][...] = full[...]


def project(size, halves, where, ends, starts, w_out_t, parts):
    width, depth = w_out_t.shape
    requests = ends.shape[1]
    outs = tuple(jax.ShapeDtypeStruct((width // halves, requests), F32) for _ in range(halves))
    return pl.pallas_call(
        functools.partial(project_kernel, size, halves),
        out_shape=outs,
        in_specs=[SMEM] + [VMEM] * (3 + len(parts)),
        out_specs=tuple(VMEM for _ in outs),
        scratch_shapes=[pltpu.VMEM((depth, requests), BF), pltpu.VMEM((width, requests), F32)],
        compiler_params=params(24),
        cost_estimate=SMALL,
        name="project",
    )(where, ends, starts, w_out_t, *parts)


def stream_kernel(halves, place_ref, res_ref, gain_ref, *refs):
    terms, (hidden_ref, msg_ref) = refs[:-2], refs[-2:]
    n = hidden_ref.shape[0]
    first = pl.multiple_of(place_ref[1] * n, 16) if halves == 2 else 0
    hidden = res_ref[pl.ds(first, n), :].astype(F32)
    for term in terms:
        hidden = hidden + term[...]
    hidden_ref[...] = hidden
    msg_ref[:n, :] = (hidden * gain_ref[pl.ds(first, n), :]).astype(BF)
    squares = jnp.sum(hidden * hidden, axis=0, keepdims=True)
    row = lax.broadcasted_iota(jnp.int32, (STAT, hidden.shape[1]), 0)
    stat = jnp.zeros((STAT, hidden.shape[1]), F32)
    for j, part in enumerate(three(squares)):
        stat = jnp.where(row == j, part, stat)
    msg_ref[n:, :] = stat.astype(BF)


def stream(halves, where, residual_t, gain_wide, terms):
    n, requests = terms[0].shape
    return pl.pallas_call(
        functools.partial(stream_kernel, halves),
        out_shape=(jax.ShapeDtypeStruct((n, requests), F32), jax.ShapeDtypeStruct((n + STAT, requests), BF)),
        in_specs=[SMEM] + [VMEM] * (2 + len(terms)),
        out_specs=(VMEM, VMEM),
        cost_estimate=SMALL,
        name="stream",
    )(where, residual_t, gain_wide, *terms)


def swiglu_kernel(size, halves, chunk, place_ref, gate_any, up_any, down_any, *refs):
    n_in = len(strides(size)[1])
    msgs = [refs[h * n_in:(h + 1) * n_in] for h in range(halves)]
    outs = [refs[(halves + h) * n_in:(halves + h + 1) * n_in] for h in range(halves)]
    gate, up, down, x, xt, acc_g, acc_u, h_scr, full, sem = refs[2 * halves * n_in:]
    width, units = gate.shape
    requests = x.shape[1]
    pieces = width // chunk
    n_outer = len(strides(size)[0])
    own, half = place_ref[0], place_ref[1]
    n = msgs[0][0].shape[1] - STAT

    def copies(i):
        at = pl.ds(i * chunk if isinstance(i, int) else pl.multiple_of(i * chunk, chunk), chunk)
        return (pltpu.make_async_copy(gate_any.at[at], gate.at[at], sem.at[0, i]),
                pltpu.make_async_copy(up_any.at[at], up.at[at], sem.at[1, i]))

    def down_copy(i):
        at = pl.ds(i * chunk if isinstance(i, int) else pl.multiple_of(i * chunk, chunk), chunk)
        return pltpu.make_async_copy(down_any.at[:, at], down.at[:, at], sem.at[2, i])

    for i in range(pieces):
        for c in copies(i):
            c.start()
    for i in range(pieces):
        down_copy(i).start()

    squares = jnp.zeros((1, requests), F32)
    for h in range(halves):
        side = half if h == 0 else 1 - half
        for k in range(n_in):
            for j in range(n_outer):
                s = relative(size, own, k * n_outer + j)
                at = s * (n * halves) + (side * n if halves == 2 else 0)
                x[pl.ds(pl.multiple_of(at, 16), n), :] = msgs[h][k][j, :n, :]
                stat = msgs[h][k][j, n:, :].astype(F32)
                squares = squares + jnp.sum(stat, axis=0, keepdims=True)
    scale = lax.rsqrt(squares / width + 1e-05)
    column = jnp.transpose(jnp.broadcast_to(scale, (requests, requests)))[:, :1]
    for i in range(width // LANE):
        xt[:, i * LANE:(i + 1) * LANE] = jnp.transpose(x[i * LANE:(i + 1) * LANE, :])
    acc_g[...] = jnp.zeros_like(acc_g)
    acc_u[...] = jnp.zeros_like(acc_u)

    def lap(i, carry):
        for c in copies(i):
            c.wait()
        at = pl.ds(pl.multiple_of(i * chunk, chunk), chunk)
        acc_g[...] += jnp.dot(xt[:, at], gate[at, :], preferred_element_type=F32)
        acc_u[...] += jnp.dot(xt[:, at], up[at, :], preferred_element_type=F32)
        return carry

    lax.fori_loop(0, pieces, lap, 0)
    g = acc_g[...] * column
    h_scr[...] = (g / (1.0 + jnp.exp(-g)) * (acc_u[...] * column)).astype(BF)

    def lap_down(i, carry):
        down_copy(i).wait()
        at = pl.ds(pl.multiple_of(i * chunk, chunk), chunk)
        full[at, :] = jnp.transpose(jnp.dot(h_scr[...], down[:, at], preferred_element_type=F32))
        return carry

    lax.fori_loop(0, pieces, lap_down, 0)
    for h in range(halves):
        side = half if h == 0 else 1 - half
        for k in range(n_in):
            for j in range(n_outer):
                s = relative(size, own, k * n_outer + j)
                at = s * (n * halves) + (side * n if halves == 2 else 0)
                outs[h][k][j] = full[pl.ds(pl.multiple_of(at, 8), n), :].astype(outs[h][k].dtype)


def swiglu(size, halves, where, w_gate, w_up, w_down, messages):
    outer, inner = strides(size)
    width, units = w_gate.shape
    requests = messages[0].shape[-1]
    n = messages[0].shape[1] - STAT
    chunk = 512
    outs = tuple(
        jax.ShapeDtypeStruct((len(outer), n, requests), F32 if h == 0 else BF) for h in range(halves) for _ in inner
    )
    return pl.pallas_call(
        functools.partial(swiglu_kernel, size, halves, chunk),
        out_shape=outs,
        in_specs=[SMEM, ANY, ANY, ANY] + [VMEM] * len(messages),
        out_specs=tuple(VMEM for _ in outs),
        scratch_shapes=[
            pltpu.VMEM((width, units), BF),
            pltpu.VMEM((width, units), BF),
            pltpu.VMEM((units, width), BF),
            pltpu.VMEM((width, requests), BF),
            pltpu.VMEM((requests, width), BF),
            pltpu.VMEM((requests, units), F32),
            pltpu.VMEM((requests, units), F32),
            pltpu.VMEM((requests, units), BF),
            pltpu.VMEM((width, requests), F32),
            pltpu.SemaphoreType.DMA((3, width // chunk)),
        ],
        compiler_params=params(56),
        cost_estimate=SMALL,
        name="swiglu",
    )(where, w_gate, w_up, w_down, *messages)


def shards(
    kv_cache,
    keep_list,
    drop_level,
    drop_table,
    req_blocks,
    tenant_sizes,
    queries,
    residual,
    w_out,
    norm_gain,
    w_gate,
    w_up,
    w_down,
):
    entries, kvl, _ = kv_cache.shape
    requests = queries.shape[0]
    size = lax.axis_size("seq")
    mp = lax.axis_size("mp")
    halves = 2 if mp == 2 else 1
    own = lax.axis_index("seq")
    half = lax.axis_index("mp")
    where = jnp.stack([own, half]).astype(jnp.int32)
    nb = entries // BLK
    slots = entries // 2
    chunk = slots // size
    keep = keep_list.reshape(nb, BLK)
    level = drop_level.reshape(nb, BLK)
    by_entry = kv_cache.reshape(entries, kvl, 2, LANE).transpose(0, 2, 1, 3).reshape(entries, 2 * kvl, LANE)
    by_row = by_entry.reshape(entries * 2 * kvl, LANE)
    outer, inner = strides(size)
    n_outer, n_inner = len(outer), len(inner)

    kept = jnp.sum(keep, axis=0, keepdims=True)
    near_counts = gather_near(kept, size)
    counts = gather_far(near_counts, size)

    partial, summaries, rank = attend(
        where, req_blocks, tenant_sizes, drop_table, by_row, keep, level, queries, kvl
    )
    gain_wide = jnp.broadcast_to(norm_gain[:, None], (norm_gain.shape[0], requests))
    near_parts = after(gather_near(after(partial, near_counts), size), counts)
    parts = gather_far(near_parts, size)

    early = chunk * 7 // 16
    late = chunk - early
    *pieces, totals = compact(size, early, late, where, rank, after(counts, near_parts), by_entry)
    entry = (2 * kvl, LANE)

    def over(values, distances):
        return [value if d == 0 else swap(value, "seq", size, d) for value, d in zip(values, distances)]

    first_a = over([p.reshape(n_inner, early, *entry) for p in pieces[:n_outer]], outer)
    first_b = over([p.reshape(n_outer, late, *entry) for p in after(pieces[n_outer:], parts)], inner)
    second_a, second_b = regroup(first_a), regroup(first_b)
    early_in, late_in = over(second_a, inner), over(second_b, outer)
    packed = place(size, where, early_in, late_in, totals)
    packed = packed.reshape(slots, 2, kvl, LANE).transpose(0, 2, 1, 3).reshape(1, slots, kvl, 2 * LANE)

    request_ids = jnp.arange(requests, dtype=jnp.int32)
    ends = jnp.sum(jnp.where(request_ids[None, :] <= request_ids[:, None], req_blocks[None, :], 0), axis=1)
    starts = ends - req_blocks

    terms = project(size, halves, where, ends.reshape(1, -1), starts.reshape(1, -1), w_out.T, after(parts, gain_wide))
    if halves == 2:
        terms = (terms[0], swap(terms[1], "mp", 2, 1))
    else:
        terms = (lax.psum(terms[0], "mp"),)
    hidden, message = stream(halves, where, residual.T, gain_wide, after(terms, first_a))

    near_message = after(gather_near(message, size), second_a, second_b)
    messages = gather_far(near_message, size)
    if halves == 2:
        messages = messages + [swap(m, "mp", 2, 1) for m in messages]
    outs = swiglu(size, halves, where, w_gate, w_up, w_down, messages)
    n_in = len(outs) // halves
    outs = after(outs, early_in, late_in)
    if halves == 2:
        sums = [(mine + swap(theirs, "mp", 2, 1).astype(F32)).astype(BF) for mine, theirs in zip(outs[:n_in], outs[n_in:])]
    else:
        sums = [mine.astype(BF) for mine in outs]
    near = sums[0].astype(F32)
    for k in inner[1:]:
        near = near + swap(sums[k], "seq", size, k).astype(F32)
    sent = after(near.astype(BF), packed)
    down = near[0]
    for j, d in list(enumerate(outer))[1:]:
        down = down + swap(sent[j], "seq", size, d).astype(F32)
    if halves == 2:
        final = (hidden + down).astype(BF)
        other = swap(final, "mp", 2, 1)
        final = jnp.concatenate([jnp.where(half == 0, final, other), jnp.where(half == 0, other, final)], axis=0)
    else:
        down = lax.psum(down.astype(BF), "mp").astype(F32)
        final = (hidden + down).astype(BF)
    return (summaries, packed, final.T)


def solution(mesh):
    placed = (
        P("seq", "mp", None),
        P("seq"),
        P("seq"),
        P(),
        P(),
        P(),
        P(None, "mp", None),
        P(None, "seq"),
        P("mp", "seq"),
        P("seq"),
        P(None, ("seq", "mp")),
        P(None, ("seq", "mp")),
        P(("seq", "mp"), None),
    )
    return jax.shard_map(
        shards,
        mesh=mesh,
        in_specs=placed,
        out_specs=(P("seq", "mp", None), P("seq", None, "mp", None), P(None, "seq")),
        check_vma=False,
    )
```

```python
import functools
import math

import jax
import jax.numpy as jnp
from jax import lax
from jax.experimental import pallas as pl
from jax.experimental.pallas import tpu as pltpu
from jax.sharding import PartitionSpec as P

BLK = 128
LANE = 128
STAT = 16
BF = jnp.bfloat16
F32 = jnp.float32
VMEM = pl.BlockSpec(memory_space=pltpu.VMEM)
SMEM = pl.BlockSpec(memory_space=pltpu.SMEM)
ANY = pl.BlockSpec(memory_space=pl.ANY)
MIB = 1 << 20
SMALL = pl.CostEstimate(flops=0, bytes_accessed=1024, transcendentals=0)


def params(mib):
    return pltpu.CompilerParams(vmem_limit_bytes=mib * MIB)


def three(value):
    hi = value.astype(BF).astype(F32)
    mid = (value - hi).astype(BF).astype(F32)
    lo = (value - hi - mid).astype(BF).astype(F32)
    return hi, mid, lo


def attend_kernel(kvl, place_ref, req_ref, ten_ref, table, kv_any, keep_ref, level_ref, q_ref,
                  o_ref, sum_ref, rank_ref, kv, s_scr, left, out_scr, o_scr, sum_scr, breq, sem):
    nb = keep_ref.shape[0]
    requests, heads = q_ref.shape[0], q_ref.shape[1]
    groups = heads // kvl
    rpe = 2 * kvl
    rows = BLK * rpe
    tenants, levels = table.shape
    copies = []
    for b in range(nb):
        c = pltpu.make_async_copy(kv_any.at[pl.ds(b * rows, rows)], kv.at[pl.ds(b * rows, rows)], sem.at[b])
        c.start()
        copies.append(c)
    first = place_ref[0] * nb

    def owned(r, begin):
        end = begin + req_ref[r]

        def mark(b, carry):
            breq[b] = r
            return carry

        lax.fori_loop(jnp.maximum(begin - first, 0), jnp.minimum(end - first, nb), mark, 0)
        return end

    lax.fori_loop(0, requests, owned, jnp.int32(0))
    scale = 1.0 / math.sqrt(LANE)
    for b in range(nb):
        copies[b].wait()
        s_scr[b * heads:(b + 1) * heads, :] = lax.dot_general(
            q_ref[breq[b]], kv[b * rows:(b + 1) * rows, :], (((1,), (1,)), ((), ())), preferred_element_type=F32
        )
    keep = keep_ref[...]
    keep_f = keep.astype(F32)
    up = (lax.broadcasted_iota(jnp.int32, (BLK, BLK), 0) <= lax.broadcasted_iota(jnp.int32, (BLK, BLK), 1))
    within = jnp.dot(keep_f.astype(BF), up.astype(F32).astype(BF), preferred_element_type=F32)
    count = jnp.broadcast_to(jnp.sum(keep_f, axis=1, keepdims=True), (nb, BLK))
    before = jnp.zeros((nb, BLK), F32)
    row_id = lax.broadcasted_iota(jnp.int32, (nb, BLK), 0)
    for b in range(nb - 1):
        before = before + jnp.where(row_id > b, count[b:b + 1], 0.0)
    rank_ref[...] = jnp.where(keep == 1, (within + before).astype(jnp.int32) - 1, -1)
    weights = []
    for b in range(nb):
        request = breq[b]
        end, tenant = ten_ref[0], jnp.int32(0)
        for t in range(1, tenants):
            tenant = tenant + (request >= end).astype(jnp.int32)
            end = end + ten_ref[t]
        level = level_ref[b:b + 1, :]
        w = jnp.zeros((1, BLK), F32)
        for j in range(levels):
            w = jnp.where(level == j, table[tenant, j], w)
        weights.append(w)
    weight = jnp.where(keep == 1, 0.0, jnp.concatenate(weights, axis=0)).astype(BF)
    mass = jnp.sum(weight.astype(F32), axis=1, keepdims=True)
    log_mass = jnp.log(mass)
    spread = (lax.broadcasted_iota(jnp.int32, (BLK, rows), 1) // rpe
              == lax.broadcasted_iota(jnp.int32, (BLK, rows), 0)).astype(F32).astype(BF)
    wide = jnp.dot(jnp.concatenate([keep_f.astype(BF), weight], axis=0), spread, preferred_element_type=F32)
    lane_in = lax.broadcasted_iota(jnp.int32, (heads, rows), 1) % rpe
    head_of = lax.broadcasted_iota(jnp.int32, (heads, rows), 0) // groups
    is_key = lane_in == head_of
    is_value = lane_in == head_of + kvl
    tops, totals = [], []
    for b in range(nb):
        s = jnp.where(is_key & (wide[b:b + 1] > 0.5), s_scr[b * heads:(b + 1) * heads, :] * scale, -1e30)
        m = jnp.max(s, axis=1, keepdims=True)
        p = jnp.exp(s - m)
        tops.append(m)
        totals.append(jnp.sum(p, axis=1, keepdims=True))
        p = pltpu.roll(p, kvl, 1)
        p_hi = p.astype(BF)
        w_row = wide[nb + b:nb + b + 1]
        left[b, :heads] = p_hi
        left[b, heads:2 * heads] = (p - p_hi.astype(F32)).astype(BF)
        left[b, 2 * heads:3 * heads] = jnp.where(is_key, w_row, 0.0).astype(BF)
        left[b, 3 * heads:] = jnp.where(is_value, w_row, 0.0).astype(BF)
    for b in range(nb):
        out_scr[b] = jnp.dot(left[b], kv[b * rows:(b + 1) * rows, :], preferred_element_type=F32)
    lse_all = jnp.zeros((heads, LANE), F32)
    lane_id = lax.broadcasted_iota(jnp.int32, (heads, LANE), 1)
    for b in range(nb):
        m, total = tops[b], totals[b]
        o = out_scr[b, :heads] + out_scr[b, heads:2 * heads]
        s_key = (out_scr[b, 2 * heads:3 * heads] / mass[b:b + 1]).astype(BF).astype(F32)
        s_val = (out_scr[b, 3 * heads:] / mass[b:b + 1]).astype(BF).astype(F32)
        s_score = jnp.sum(q_ref[breq[b]].astype(F32) * s_key, axis=1, keepdims=True) * scale + log_mass[b:b + 1]
        top = jnp.maximum(m, s_score)
        a = jnp.exp(m - top)
        e = jnp.exp(s_score - top)
        total = total * a + e
        o_scr[:, b, :] = (o * a + s_val * e) / total
        lse_all = jnp.where(lane_id == b, top + jnp.log(total), lse_all)
        for h in range(kvl):
            sum_scr[b, h:h + 1, :LANE] = s_key[h * groups:h * groups + 1]
            sum_scr[b, h:h + 1, LANE:] = s_val[h * groups:h * groups + 1]
    o_ref[:heads] = o_scr[...].astype(BF)
    sum_ref[...] = sum_scr[...].astype(BF)
    square = jnp.concatenate([lse_all, jnp.zeros((LANE - heads, LANE), F32)], axis=0)
    lse = jnp.transpose(square)[:nb]
    hi, mid, lo = three(lse)
    o_ref[heads] = (hi + pltpu.roll(mid, 32, 1) + pltpu.roll(lo, 64, 1)).astype(BF)


def attend(where, req_blocks, tenant_sizes, table, kv_rows, keep, level, queries, kvl):
    nb = keep.shape[0]
    heads = queries.shape[1]
    rows = BLK * 2 * kvl
    return pl.pallas_call(
        functools.partial(attend_kernel, kvl),
        out_shape=(
            jax.ShapeDtypeStruct((heads + 1, nb, LANE), BF),
            jax.ShapeDtypeStruct((nb, kvl, 2 * LANE), BF),
            jax.ShapeDtypeStruct((nb, BLK), jnp.int32),
        ),
        in_specs=[SMEM, SMEM, SMEM, SMEM, ANY, VMEM, VMEM, VMEM],
        out_specs=(VMEM, VMEM, VMEM),
        scratch_shapes=[
            pltpu.VMEM(kv_rows.shape, BF),
            pltpu.VMEM((nb * heads, rows), F32),
            pltpu.VMEM((nb, 4 * heads, rows), BF),
            pltpu.VMEM((nb, 4 * heads, LANE), F32),
            pltpu.VMEM((heads, nb, LANE), F32),
            pltpu.VMEM((nb, kvl, 2 * LANE), F32),
            pltpu.SMEM((nb,), jnp.int32),
            pltpu.SemaphoreType.DMA((nb,)),
        ],
        compiler_params=params(60),
        cost_estimate=pl.CostEstimate(flops=nb * 2 * 80 * 1024 * 128, bytes_accessed=5 * MIB, transcendentals=nb * 16384),
        name="attend",
    )(where, req_blocks, tenant_sizes, table, kv_rows, keep, level, queries)


def shift(value, size):
    return lax.shift_right_logical(value, jnp.int32(size.bit_length() - 1))


def compact_kernel(size, early, late, place_ref, rank_ref, kv_any, *refs):
    count_refs, refs = refs[:len(strides(size)[1])], refs[len(strides(size)[1]):]
    outs, total_ref, (kv, out, dst_v, dst, sem, out_sem, dst_sem) = refs[:-8], refs[-8], refs[-7:]
    nb = rank_ref.shape[0]
    n_outer, n_inner = (len(d) for d in strides(size))
    own = place_ref[0]
    for b in range(nb):
        pltpu.make_async_copy(kv_any.at[pl.ds(b * BLK, BLK)], kv.at[pl.ds(b * BLK, BLK)], sem.at[b]).start()
    by_lane = jnp.concatenate([ref[j] for ref in count_refs for j in range(ref.shape[0])], axis=0).astype(F32)
    counts = jnp.broadcast_to(jnp.sum(by_lane, axis=1, keepdims=True), (size, LANE))
    total_ref[...] = counts.astype(jnp.int32)
    source = relative(size, own, lax.broadcasted_iota(jnp.int32, (size, LANE), 0))
    offset = jnp.sum(jnp.where(source < own, counts, 0.0), axis=0, keepdims=True).astype(jnp.int32)
    rank = rank_ref[...]
    position = offset + jnp.maximum(rank, 0)
    owner = position & (size - 1)
    slot = shift(position, size) - shift(offset + (size - 1) - owner, size)
    apart = owner ^ own
    k, j = apart & (n_inner - 1), shift(apart, n_inner)
    first = (j * n_inner + k) * early + slot
    second = size * early + (k * n_outer + j) * late + slot - early
    dst_v[...] = jnp.where(rank >= 0, jnp.where(slot < early, first, second), size * (early + late))
    to_scalars = pltpu.make_async_copy(dst_v, dst, dst_sem)
    to_scalars.start()
    to_scalars.wait()

    def one(b, carry):
        pltpu.make_async_copy(kv_any.at[pl.ds(b * BLK, BLK)], kv.at[pl.ds(b * BLK, BLK)], sem.at[b]).wait()
        for i in range(BLK):
            out[dst[b, i]] = kv[b * BLK + i]
        return carry

    lax.fori_loop(0, nb, one, 0)
    copies, at = [], 0
    for j, ref in enumerate(outs):
        copies.append(pltpu.make_async_copy(out.at[pl.ds(at, ref.shape[0])], ref, out_sem.at[j]))
        at += ref.shape[0]
    for copy in copies:
        copy.start()
    for copy in copies:
        copy.wait()


def compact(size, early, late, where, rank, counts, kv_entries):
    nb = rank.shape[0]
    rpe = kv_entries.shape[1]
    n_outer, n_inner = (len(d) for d in strides(size))
    lengths = [n_inner * early] * n_outer + [n_outer * late] * n_inner
    return pl.pallas_call(
        functools.partial(compact_kernel, size, early, late),
        out_shape=tuple(jax.ShapeDtypeStruct((n, rpe, LANE), BF) for n in lengths)
        + (jax.ShapeDtypeStruct((size, LANE), jnp.int32),),
        in_specs=[SMEM, VMEM, ANY] + [VMEM] * len(counts),
        out_specs=(ANY,) * len(lengths) + (VMEM,),
        scratch_shapes=[
            pltpu.VMEM(kv_entries.shape, BF),
            pltpu.VMEM((sum(lengths) + 8, rpe, LANE), BF),
            pltpu.VMEM((nb, BLK), jnp.int32),
            pltpu.SMEM((nb, BLK), jnp.int32),
            pltpu.SemaphoreType.DMA((nb,)),
            pltpu.SemaphoreType.DMA((len(lengths),)),
            pltpu.SemaphoreType.DMA,
        ],
        compiler_params=params(60),
        cost_estimate=SMALL,
        name="compact",
    )(where, rank, kv_entries, *counts)


def regroup_kernel(n, *refs):
    ins, outs, held, sem, out_sem = refs[:n], refs[n:-3], refs[-3], refs[-2], refs[-1]
    m = len(outs)
    copies = [[pltpu.make_async_copy(ref.at[i], held.at[i, j], sem.at[j, i]) for j, ref in enumerate(ins)] for i in range(m)]
    for row in copies:
        for copy in row:
            copy.start()
    sends = []
    for i, row in enumerate(copies):
        for copy in row:
            copy.wait()
        sends.append(pltpu.make_async_copy(held.at[i], outs[i], out_sem.at[i]))
        sends[-1].start()
    for copy in sends:
        copy.wait()


def regroup(values):
    n, m = len(values), values[0].shape[0]
    return pl.pallas_call(
        functools.partial(regroup_kernel, n),
        out_shape=(jax.ShapeDtypeStruct((n, *values[0].shape[1:]), values[0].dtype),) * m,
        in_specs=[ANY] * n,
        out_specs=(ANY,) * m,
        scratch_shapes=[
            pltpu.VMEM((m, n, *values[0].shape[1:]), values[0].dtype),
            pltpu.SemaphoreType.DMA((n, m)),
            pltpu.SemaphoreType.DMA((m,)),
        ],
        compiler_params=params(6),
        cost_estimate=SMALL,
        name="regroup",
    )(*values)


def place_kernel(size, n_inner, place_ref, count, *refs):
    parts, (out_any, got, out, sem, out_sem) = refs[:-5], refs[-5:]
    early = parts[0].shape[1]
    chunk = got.shape[2]
    slots = out_any.shape[0]
    copies = []
    for i, part in enumerate(parts):
        if i < n_inner:
            to = got.at[i, :, pl.ds(0, early)]
        else:
            to = got.at[:, i - n_inner, pl.ds(early, chunk - early)]
        c = pltpu.make_async_copy(part, to, sem.at[i])
        c.start()
        copies.append(c)
    blank = jnp.zeros(out.shape[1:], out.dtype)

    def clear(i, carry):
        for j in range(16):
            out[i * 16 + j] = blank
        return carry

    lax.fori_loop(slots // 2 // 16, slots // 16, clear, 0)
    for c in copies:
        c.wait()

    own = place_ref[0]

    def source(s, before):
        apart = own ^ s
        k, j = apart & (n_inner - 1), shift(apart, n_inner)
        base = shift(before + (size - 1) - own, size)
        for i in range(chunk):
            out[base + i] = got[k, j, i]
        return before + count[k * got.shape[1] + j, 0]

    filled = shift(lax.fori_loop(0, size, source, jnp.int32(0)) + (size - 1) - own, size)
    for i in range(chunk):
        out[filled + i] = blank
    copy = pltpu.make_async_copy(out.at[pl.ds(0, slots)], out_any, out_sem)
    copy.start()
    copy.wait()


def place(size, where, early, late, counts):
    n_outer, n_inner = len(late), len(early)
    rpe = early[0].shape[2]
    chunk = early[0].shape[1] + late[0].shape[1]
    slots = size * chunk
    return pl.pallas_call(
        functools.partial(place_kernel, size, n_inner),
        out_shape=jax.ShapeDtypeStruct((slots, rpe, LANE), BF),
        in_specs=[SMEM, SMEM] + [ANY] * (n_outer + n_inner),
        out_specs=ANY,
        scratch_shapes=[
            pltpu.VMEM((n_inner, n_outer, chunk, rpe, LANE), BF),
            pltpu.VMEM((slots + chunk, rpe, LANE), BF),
            pltpu.SemaphoreType.DMA((n_inner + n_outer,)),
            pltpu.SemaphoreType.DMA,
        ],
        compiler_params=params(12),
        cost_estimate=SMALL,
        name="place",
    )(where, counts, *early, *late)


def strides(size):
    inner = max(size // 4, 1)
    return [j * inner for j in range(size // inner)], list(range(inner))


def swap(value, axis, size, distance):
    return lax.ppermute(value, axis, [(i, i ^ distance) for i in range(size)])


def gather_near(value, size):
    return jnp.stack([value if d == 0 else swap(value, "seq", size, d) for d in strides(size)[0]])


def gather_far(near, size):
    return [near if k == 0 else swap(near, "seq", size, k) for k in strides(size)[1]]


def after(value, *others):
    return lax.optimization_barrier((value, others))[0]


def relative(size, own, position):
    outer, inner = strides(size)
    n = len(outer)
    return own ^ ((position % n) * len(inner)) ^ (position // n)


def project_kernel(size, halves, place_ref, req_ref, w_ref, *refs):
    parts = refs[:len(strides(size)[1])]
    outs, (att, full) = refs[len(parts):-2], refs[-2:]
    heads = parts[0].shape[1] - 1
    nb = parts[0].shape[2]
    blocks = size * nb
    requests = req_ref.shape[1]
    own, half = place_ref[0], place_ref[1]
    at = lax.broadcasted_iota(jnp.int32, (blocks, requests), 0)
    ids = relative(size, own, at // nb) * nb + at % nb
    lengths = jnp.broadcast_to(req_ref[...].astype(F32), (16, requests)).astype(BF)
    upto = (lax.broadcasted_iota(jnp.int32, (requests, requests), 0) <= lax.broadcasted_iota(jnp.int32, (requests, requests), 1))
    ends = jnp.dot(lengths, upto.astype(F32).astype(BF), preferred_element_type=F32)[:1].astype(jnp.int32)
    member = (ids >= ends - req_ref[...]) & (ids < ends)
    packed = jnp.concatenate([part[:, heads].reshape(-1, LANE) for part in parts], axis=0).astype(F32)
    lse = packed + pltpu.roll(packed, LANE - 32, 1) + pltpu.roll(packed, LANE - 64, 1)
    for g in range(heads):
        column = jnp.where(member, lse[:, g:g + 1], -1e30)
        top = jnp.max(column, axis=0, keepdims=True)
        weight = jnp.where(member, jnp.exp(column - top), 0.0).astype(BF)
        total = jnp.sum(weight.astype(F32), axis=0, keepdims=True)
        o = jnp.concatenate([part[:, g].reshape(-1, LANE) for part in parts], axis=0)
        mixed = lax.dot_general(o, weight, (((0,), (0,)), ((), ())), preferred_element_type=F32)
        att[g * LANE:(g + 1) * LANE, :] = (mixed / total).astype(BF)
    full[...] = jnp.dot(w_ref[...], att[...], preferred_element_type=F32)
    if halves == 2:
        n = full.shape[0] // 2
        outs[0][...] = full[pl.ds(pl.multiple_of(half * n, 8), n), :]
        outs[1][...] = full[pl.ds(pl.multiple_of((1 - half) * n, 8), n), :]
    else:
        outs[0][...] = full[...]


def project(size, halves, where, req_row, w_out_t, parts):
    width, depth = w_out_t.shape
    requests = req_row.shape[1]
    outs = tuple(jax.ShapeDtypeStruct((width // halves, requests), F32) for _ in range(halves))
    return pl.pallas_call(
        functools.partial(project_kernel, size, halves),
        out_shape=outs,
        in_specs=[SMEM] + [VMEM] * (2 + len(parts)),
        out_specs=tuple(VMEM for _ in outs),
        scratch_shapes=[pltpu.VMEM((depth, requests), BF), pltpu.VMEM((width, requests), F32)],
        compiler_params=params(12),
        cost_estimate=SMALL,
        name="project",
    )(where, req_row, w_out_t, *parts)


def stream_kernel(halves, place_ref, res_ref, gain_ref, *refs):
    terms, (hidden_ref, msg_ref, gain) = refs[:-3], refs[-3:]
    n = hidden_ref.shape[0]
    first = pl.multiple_of(place_ref[1] * n, 16) if halves == 2 else 0
    hidden = res_ref[pl.ds(first, n), :].astype(F32)
    for term in terms:
        hidden = hidden + term[...]
    hidden_ref[...] = hidden
    width = gain_ref.shape[1]
    row = jnp.concatenate([gain_ref[...], jnp.zeros((1, -width % LANE), F32)], axis=1)
    gain[...] = jnp.transpose(jnp.broadcast_to(row, (hidden.shape[1], row.shape[1])))
    msg_ref[:n, :] = (hidden * gain[pl.ds(first, n), :]).astype(BF)
    squares = jnp.sum(hidden * hidden, axis=0, keepdims=True)
    row = lax.broadcasted_iota(jnp.int32, (STAT, hidden.shape[1]), 0)
    stat = jnp.zeros((STAT, hidden.shape[1]), F32)
    for j, part in enumerate(three(squares)):
        stat = jnp.where(row == j, part, stat)
    msg_ref[n:, :] = stat.astype(BF)


def stream(halves, where, residual_t, gain, terms):
    n, requests = terms[0].shape
    return pl.pallas_call(
        functools.partial(stream_kernel, halves),
        out_shape=(jax.ShapeDtypeStruct((n, requests), F32), jax.ShapeDtypeStruct((n + STAT, requests), BF)),
        in_specs=[SMEM] + [VMEM] * (2 + len(terms)),
        out_specs=(VMEM, VMEM),
        scratch_shapes=[pltpu.VMEM((-(-gain.shape[1] // LANE) * LANE, requests), F32)],
        compiler_params=params(6),
        cost_estimate=SMALL,
        name="stream",
    )(where, residual_t, gain, *terms)


def gate_up_kernel(size, halves, chunk, place_ref, gate, up, *refs):
    n_in = len(strides(size)[1])
    msgs = [refs[h * n_in:(h + 1) * n_in] for h in range(halves)]
    h_ref, x, xt, acc_g, acc_u = refs[halves * n_in:]
    width, units = gate.shape
    requests = x.shape[1]
    n_outer = len(strides(size)[0])
    own, half = place_ref[0], place_ref[1]
    n = msgs[0][0].shape[1] - STAT
    squares = jnp.zeros((1, requests), F32)
    for h in range(halves):
        side = half if h == 0 else 1 - half
        for k in range(n_in):
            for j in range(n_outer):
                s = relative(size, own, k * n_outer + j)
                at = s * (n * halves) + (side * n if halves == 2 else 0)
                x[pl.ds(pl.multiple_of(at, 16), n), :] = msgs[h][k][j, :n, :]
                stat = msgs[h][k][j, n:, :].astype(F32)
                squares = squares + jnp.sum(stat, axis=0, keepdims=True)
    scale = lax.rsqrt(squares / width + 1e-05)
    column = jnp.transpose(jnp.broadcast_to(scale, (requests, requests)))[:, :1]
    for i in range(width // LANE):
        xt[:, i * LANE:(i + 1) * LANE] = jnp.transpose(x[i * LANE:(i + 1) * LANE, :])
    acc_g[...] = jnp.zeros_like(acc_g)
    acc_u[...] = jnp.zeros_like(acc_u)

    def lap(i, carry):
        at = pl.ds(pl.multiple_of(i * chunk, chunk), chunk)
        acc_g[...] += jnp.dot(xt[:, at], gate[at, :], preferred_element_type=F32)
        acc_u[...] += jnp.dot(xt[:, at], up[at, :], preferred_element_type=F32)
        return carry

    lax.fori_loop(0, width // chunk, lap, 0)
    g = acc_g[...] * column
    h_ref[...] = (g / (1.0 + jnp.exp(-g)) * (acc_u[...] * column)).astype(BF)


def down_kernel(size, halves, chunk, place_ref, h_ref, down, *refs):
    n_in = len(strides(size)[1])
    outs, full = [refs[h * n_in:(h + 1) * n_in] for h in range(halves)], refs[-1]
    width = down.shape[1]
    n_outer = len(strides(size)[0])
    own, half = place_ref[0], place_ref[1]
    n = outs[0][0].shape[1]

    def lap_down(i, carry):
        at = pl.ds(pl.multiple_of(i * chunk, chunk), chunk)
        full[at, :] = jnp.transpose(jnp.dot(h_ref[...], down[:, at], preferred_element_type=F32))
        return carry

    lax.fori_loop(0, width // chunk, lap_down, 0)
    for h in range(halves):
        side = half if h == 0 else 1 - half
        for k in range(n_in):
            for j in range(n_outer):
                s = relative(size, own, k * n_outer + j)
                at = s * (n * halves) + (side * n if halves == 2 else 0)
                outs[h][k][j] = full[pl.ds(pl.multiple_of(at, 8), n), :].astype(outs[h][k].dtype)


def swiglu(size, halves, where, w_gate, w_up, w_down, messages):
    outer, inner = strides(size)
    width, units = w_gate.shape
    requests = messages[0].shape[-1]
    n = messages[0].shape[1] - STAT
    chunk = 512
    hidden = pl.pallas_call(
        functools.partial(gate_up_kernel, size, halves, chunk),
        out_shape=jax.ShapeDtypeStruct((requests, units), BF),
        in_specs=[SMEM] + [VMEM] * (2 + len(messages)),
        out_specs=VMEM,
        scratch_shapes=[
            pltpu.VMEM((width, requests), BF),
            pltpu.VMEM((requests, width), BF),
            pltpu.VMEM((requests, units), F32),
            pltpu.VMEM((requests, units), F32),
        ],
        compiler_params=params(29),
        cost_estimate=SMALL,
        name="gate_up",
    )(where, w_gate, w_up, *messages)
    outs = tuple(
        jax.ShapeDtypeStruct((len(outer), n, requests), F32 if h == 0 else BF) for h in range(halves) for _ in inner
    )
    return pl.pallas_call(
        functools.partial(down_kernel, size, halves, chunk),
        out_shape=outs,
        in_specs=[SMEM] + [VMEM] * 2,
        out_specs=tuple(VMEM for _ in outs),
        scratch_shapes=[pltpu.VMEM((width, requests), F32)],
        compiler_params=params(20),
        cost_estimate=SMALL,
        name="down",
    )(where, hidden, w_down)


def shards(
    kv_cache,
    keep_list,
    drop_level,
    drop_table,
    req_blocks,
    tenant_sizes,
    queries,
    residual,
    w_out,
    norm_gain,
    w_gate,
    w_up,
    w_down,
):
    entries, kvl, _ = kv_cache.shape
    requests = queries.shape[0]
    size = lax.axis_size("seq")
    mp = lax.axis_size("mp")
    halves = 2 if mp == 2 else 1
    own = lax.axis_index("seq")
    half = lax.axis_index("mp")
    where = jnp.stack([own, half]).astype(jnp.int32)
    nb = entries // BLK
    slots = entries // 2
    chunk = slots // size
    keep = keep_list.reshape(nb, BLK)
    level = drop_level.reshape(nb, BLK)
    by_entry = kv_cache.reshape(entries, kvl, 2, LANE).transpose(0, 2, 1, 3).reshape(entries, 2 * kvl, LANE)
    by_row = by_entry.reshape(entries * 2 * kvl, LANE)
    outer, inner = strides(size)
    n_outer, n_inner = len(outer), len(inner)

    kept = jnp.sum(keep, axis=0, keepdims=True)
    near_counts = gather_near(kept, size)
    counts = gather_far(near_counts, size)

    partial, summaries, rank = attend(
        where, req_blocks, tenant_sizes, drop_table, by_row, keep, level, queries, kvl
    )
    near_parts = after(gather_near(after(partial, near_counts), size), counts)
    parts = gather_far(near_parts, size)

    early = chunk * 7 // 16
    late = chunk - early
    *pieces, totals = compact(size, early, late, where, rank, after(counts, near_parts), by_entry)
    entry = (2 * kvl, LANE)

    def over(values, distances):
        return [value if d == 0 else swap(value, "seq", size, d) for value, d in zip(values, distances)]

    first_a = over([p.reshape(n_inner, early, *entry) for p in pieces[:n_outer]], outer)
    first_b = over([p.reshape(n_outer, late, *entry) for p in after(pieces[n_outer:], parts)], inner)
    second_a, second_b = regroup(first_a), regroup(first_b)
    early_in, late_in = over(second_a, inner), over(second_b, outer)
    packed = place(size, where, early_in, late_in, totals)
    packed = packed.reshape(slots, 2, kvl, LANE).transpose(0, 2, 1, 3).reshape(1, slots, kvl, 2 * LANE)

    terms = project(size, halves, where, req_blocks.reshape(1, -1), w_out.T, parts)
    if halves == 2:
        terms = (terms[0], swap(terms[1], "mp", 2, 1))
    else:
        terms = (lax.psum(terms[0], "mp"),)
    hidden, message = stream(halves, where, residual.T, norm_gain.reshape(1, -1), after(terms, first_a))

    near_message = after(gather_near(message, size), second_a, second_b)
    messages = gather_far(near_message, size)
    if halves == 2:
        messages = messages + [swap(m, "mp", 2, 1) for m in messages]
    outs = swiglu(size, halves, where, w_gate, w_up, w_down, messages)
    n_in = len(outs) // halves
    outs = after(outs, early_in, late_in)
    if halves == 2:
        sums = [(mine + swap(theirs, "mp", 2, 1).astype(F32)).astype(BF) for mine, theirs in zip(outs[:n_in], outs[n_in:])]
    else:
        sums = [mine.astype(BF) for mine in outs]
    near = sums[0].astype(F32)
    for k in inner[1:]:
        near = near + swap(sums[k], "seq", size, k).astype(F32)
    sent = after(near.astype(BF), packed)
    down = near[0]
    for j, d in list(enumerate(outer))[1:]:
        down = down + swap(sent[j], "seq", size, d).astype(F32)
    if halves == 2:
        final = (hidden + down).astype(BF)
        other = swap(final, "mp", 2, 1)
        final = jnp.concatenate([jnp.where(half == 0, final, other), jnp.where(half == 0, other, final)], axis=0)
    else:
        down = lax.psum(down.astype(BF), "mp").astype(F32)
        final = (hidden + down).astype(BF)
    return (summaries, packed, final.T)


def solution(mesh):
    placed = (
        P("seq", "mp", None),
        P("seq"),
        P("seq"),
        P(),
        P(),
        P(),
        P(None, "mp", None),
        P(None, "seq"),
        P("mp", "seq"),
        P("seq"),
        P(None, ("seq", "mp")),
        P(None, ("seq", "mp")),
        P(("seq", "mp"), None),
    )
    return jax.shard_map(
        shards,
        mesh=mesh,
        in_specs=placed,
        out_specs=(P("seq", "mp", None), P("seq", None, "mp", None), P(None, "seq")),
        check_vma=False,
    )
```
